512 devices in a mesh: ctx: 64 (over x, y_hi, z), tp: 8 (over y_lo, core).
Axes of the slice: x: 4, y: 8 (y_hi: 2, y_lo: 4; y = y_hi * 4 + y_lo), z: 8, core: 2. Of those that a mesh axis runs over, the one named last changes fastest.
Arguments:
- q_proj: bfloat16 [8192, 4096], P('ctx', 'tp'), may hold values from -6 to 6
- k_proj: bfloat16 [8192, 4096], P('ctx', 'tp'), may hold values from -6 to 6
- v_proj: bfloat16 [8192, 4096], P('ctx', 'tp'), may hold values from -6 to 6
- short_taps: float32 [3, 3, 4096], P(None, None, 'tp'), may hold values from -3.5 to 3.5
- long_filter: float32 [8192, 4096], P('ctx', 'tp'), may hold values from -1.01 to 1.01
- grad_out: bfloat16 [8192, 4096], P('ctx', 'tp'), may hold values from -1.1953125 to 1.1953125
Outputs:
- mixed: bfloat16 [8192, 4096], P('ctx', 'tp')
- grad_q: bfloat16 [8192, 4096], P('ctx', 'tp')
- grad_k: bfloat16 [8192, 4096], P('ctx', 'tp')
- grad_v: bfloat16 [8192, 4096], P('ctx', 'tp')
- grad_taps: float32 [3, 3, 4096], P(None, None, 'tp')
- grad_filter: float32 [8192, 4096], P('ctx', 'tp')
The draws below stay inside these ranges and needn't reach their ends.
All inputs are finite; a program needn't handle non-finite values.
Results may differ from the reference program's by a relative error of at most 0.0015.
Values may be sent and summed in bfloat16 or wider, within the bound.
A program may use at most 64 MiB of HBM per device.

```python
import math
import jax
import jax.numpy as jnp
from jax import lax

D = 4096
TAPS = 3
SEQ = 8192


def draw_long_filter(key, part):
    key = jax.random.fold_in(key, 7)
    key_rate, key_noise = jax.random.split(key)
    lowest = math.log(30.0)
    highest = math.log(4.0 * SEQ)
    lifetime = jnp.exp(jax.random.uniform(key_rate, (D,), jnp.float32, lowest, highest))
    lags = jnp.arange(SEQ, dtype=jnp.float32)[:, None]
    envelope = jnp.exp(-lags / lifetime[None, :]) * lax.rsqrt(jnp.minimum(lifetime, float(SEQ)))[None, :]
    noise = jnp.clip(jax.random.normal(key_noise, (SEQ, D), jnp.float32), -5.0, 5.0)
    return noise * envelope


def levels(own_key, dims, cuts, low, largest):
    loudness, own = 1.0, jax.random.fold_in(own_key, 6)
    for dim, shards_of in cuts:
        steps = jnp.exp(jax.random.uniform(jax.random.fold_in(own, dim), (shards_of,), jnp.float32, low / len(cuts), largest / len(cuts)))
        loudness = loudness * jnp.repeat(steps, dims[dim] // shards_of).reshape([-1 if axis == dim else 1 for axis in range(len(dims))])
    return loudness


def scatter_about(own_key, extent, scale, most, cuts=(), kind=jnp.bfloat16):
    result = scale * jax.random.normal(own_key, extent, jnp.float32)
    if cuts:
        result = result * levels(own_key, extent, cuts, -0.22, 0.18)
    return jnp.clip(result, -most, most).astype(kind)


def setup_inputs(seed: int = 0) -> dict:
    arg_keys = jax.random.split(jax.random.key(seed), 7)
    return {
        "q_proj": scatter_about(arg_keys[0], (SEQ, D), 1.0, 6.0, ((0, 64), (1, 8))),
        "k_proj": scatter_about(arg_keys[1], (SEQ, D), 1.0, 6.0, ((0, 64), (1, 8))),
        "v_proj": scatter_about(arg_keys[2], (SEQ, D), 1.0, 6.0, ((0, 64), (1, 8))),
        "short_taps": scatter_about(arg_keys[3], (3, TAPS, D), TAPS ** -0.5, 3.5, ((2, 8),), jnp.float32),
        "long_filter": draw_long_filter(jax.random.fold_in(arg_keys[6], 71), 0),
        "grad_out": scatter_about(arg_keys[5], (SEQ, D), 0.2, 1.1953125, ((0, 64), (1, 8))),
    }


def delay(field, lag):
    if lag == 0:
        return field
    zeros = jnp.zeros((lag, field.shape[1]), field.dtype)
    return jnp.concatenate([zeros, field[:field.shape[0] - lag]], axis=0)


def advance(field, lag):
    if lag == 0:
        return field
    zeros = jnp.zeros((lag, field.shape[1]), field.dtype)
    return jnp.concatenate([field[lag:], zeros], axis=0)


def convolve_block(inputs):
    z_block, filter_block, gy_block = inputs
    length = 2 * SEQ
    z_spec = jnp.fft.rfft(z_block, n=length, axis=0)
    h_spec = jnp.fft.rfft(filter_block, n=length, axis=0)
    g_spec = jnp.fft.rfft(gy_block, n=length, axis=0)
    y_block = jnp.fft.irfft(z_spec * h_spec, n=length, axis=0)[:SEQ]
    dz_block = jnp.fft.irfft(g_spec * jnp.conj(h_spec), n=length, axis=0)[:SEQ]
    dh_block = jnp.fft.irfft(g_spec * jnp.conj(z_spec), n=length, axis=0)[:SEQ]
    return (y_block.astype(z_block.dtype), dz_block.astype(z_block.dtype), dh_block.astype(z_block.dtype))


def to_blocks(field, width):
    count = field.shape[1] // width
    return field.reshape(SEQ, count, width).transpose(1, 0, 2)


def from_blocks(field):
    return field.transpose(1, 0, 2).reshape(SEQ, D)


def reference(q_proj, k_proj, v_proj, short_taps, long_filter, grad_out):
    streams = [q_proj.astype(jnp.float32), k_proj.astype(jnp.float32), v_proj.astype(jnp.float32)]
    featured = []
    for s in range(3):
        total = jnp.zeros_like(streams[s])
        for j in range(TAPS):
            total = total + short_taps[s, j][None, :] * delay(streams[s], j)
        featured.append(total)
    z = featured[0] * featured[2]
    grad = grad_out.astype(jnp.float32)
    gy = grad * featured[1]
    width = 512 if D % 512 == 0 else D
    y_blocks, dz_blocks, dh_blocks = lax.map(convolve_block, (to_blocks(z, width), to_blocks(long_filter, width), to_blocks(gy, width)))
    y = from_blocks(y_blocks)
    dz = from_blocks(dz_blocks)
    grad_filter = from_blocks(dh_blocks)
    mixed = (featured[1] * y).astype(jnp.bfloat16)
    deltas = [dz * featured[2], grad * y, dz * featured[0]]
    grads = []
    tap_rows = []
    for s in range(3):
        total = jnp.zeros_like(deltas[s])
        rows = []
        for j in range(TAPS):
            total = total + short_taps[s, j][None, :] * advance(deltas[s], j)
            rows.append(jnp.sum(deltas[s] * delay(streams[s], j), axis=0))
        grads.append(total.astype(jnp.bfloat16))
        tap_rows.append(jnp.stack(rows, axis=0))
    grad_taps = jnp.stack(tap_rows, axis=0)
    return (mixed, grads[0], grads[1], grads[2], grad_taps, grad_filter)
```

```python
import math

import jax
import jax.numpy as jnp
import numpy as np
from jax import lax
from jax.experimental import pallas as pl
from jax.experimental.pallas import tpu as pltpu
from jax.sharding import PartitionSpec as P

F32 = jnp.float32
BF16 = jnp.bfloat16


def split_table(table):
    hi = table.astype(BF16)
    return hi, (table - hi.astype(np.float64)).astype(BF16)


def make_tables(parts, rows):
    total = parts * rows
    k1 = np.arange(parts)
    p = np.arange(parts)
    t = np.arange(rows)
    coarse = 2.0 * math.pi * np.outer(k1 + 0.25, p) / parts
    first = np.concatenate([np.cos(coarse), -np.sin(coarse)], axis=0)
    hi, lo = split_table(first)
    first = np.concatenate([hi, hi, lo], axis=1)
    turn = 2.0 * math.pi * np.outer(k1 + 0.25, t) / total
    fine = 2.0 * math.pi * (np.outer(t, t) % rows) / rows
    second = np.block([[np.cos(fine), -np.sin(fine)], [np.sin(fine), np.cos(fine)]])
    hi, lo = split_table(second)
    second = np.concatenate([hi, hi, lo], axis=0)
    last = np.concatenate([np.cos(coarse.T), np.sin(coarse.T)], axis=1) / total
    hi, lo = split_table(last)
    last = np.concatenate([hi, hi, lo], axis=1)
    return first, second, last, np.cos(turn).astype(np.float32), -np.sin(turn).astype(np.float32)


def halves(value):
    hi = value.astype(BF16)
    return hi, (value - hi.astype(F32)).astype(BF16)


def kernel(
    q_ref, k_ref, v_ref, g_ref, h_ref, taps_ref, first_ref, second_ref, last_ref, cos_ref, sin_ref,
    mixed_ref, gq_ref, gk_ref, gv_ref, gtaps_ref, gh_ref,
    send, recv, send2, recv2, taps_t, x, feat, fields, spec, conv, lhs,
    send_sem, recv_sem, send_sem2, recv_sem2,
):
    parts, chans, rows = 64, 8, 128
    width = parts * chans
    me = lax.axis_index("ctx")
    tp = lax.axis_index("tp")
    barrier = pltpu.get_barrier_semaphore()

    def peers(body):
        def step(i, carry):
            body(jnp.bitwise_xor(me, i))
            return carry

        lax.fori_loop(1, parts, step, 0)

    def target(peer):
        return dict(device_id=(peer, tp), device_id_type=pl.DeviceIdType.MESH)

    peers(lambda peer: pl.semaphore_signal(barrier, inc=1, **target(peer)))

    def turned(ref):
        return jnp.transpose(ref[...].astype(F32)).reshape(parts, chans, rows)

    send[:, 0:16, :] = jnp.concatenate([turned(q_ref), turned(k_ref)], axis=1).astype(BF16)
    send[:, 16:32, :] = jnp.concatenate([turned(v_ref), turned(g_ref)], axis=1).astype(BF16)
    filt = turned(h_ref)
    filt_hi = filt.astype(BF16).astype(F32)
    send[:, 32:48, :] = jnp.concatenate([filt_hi, filt - filt_hi], axis=1).astype(BF16)
    taps = jnp.concatenate([taps_ref[...], jnp.zeros((rows - 9, width), F32)], axis=0)
    taps_t[...] = jnp.transpose(taps)

    pl.semaphore_wait(barrier, parts - 1)
    own = pltpu.make_async_copy(send.at[me], recv.at[me], recv_sem)
    own.start()

    def post(peer):
        pltpu.make_async_remote_copy(
            src_ref=send.at[peer], dst_ref=recv.at[me], send_sem=send_sem, recv_sem=recv_sem, **target(peer)
        ).start()

    peers(post)
    pltpu.make_async_copy(recv, recv, recv_sem).wait()

    own_taps = taps_t[pl.ds(pl.multiple_of(me * chans, chans), chans), :]

    def tap(s, j):
        return jnp.broadcast_to(own_taps[:, 3 * s + j : 3 * s + j + 1], (chans, rows))[None]

    lane = lax.broadcasted_iota(jnp.int32, (1, chans, rows), 2)
    chunk = 8

    def rolled(value, shift):
        flat = value.reshape(-1, rows)
        return pltpu.roll(flat, shift % rows, axis=1).reshape(value.shape)

    x[:, 0] = jnp.zeros((4, chans, rows), F32)

    def unpack(i, carry):
        p0 = i * chunk
        here = pl.ds(p0, chunk)
        there = pl.ds(p0 + 1, chunk)
        qk = recv[here, 0:16, :].astype(F32)
        vg = recv[here, 16:32, :].astype(F32)
        hh = recv[here, 32:48, :].astype(F32)
        x[0, there] = qk[:, 0:8]
        x[1, there] = qk[:, 8:16]
        x[2, there] = vg[:, 0:8]
        x[3, there] = vg[:, 8:16]
        fields[1, here] = hh[:, 0:8] + hh[:, 8:16]
        return carry

    lax.fori_loop(0, parts // chunk, unpack, 0)

    def delayed(s, p0):
        value = x[s, pl.ds(p0, chunk + 1)]
        out = [value[1:]]
        for j in (1, 2):
            moved = rolled(value, j)
            out.append(jnp.where(lane < j, moved[:-1], moved[1:]))
        return out

    def featurize(i, carry):
        p0 = i * chunk
        here = pl.ds(p0, chunk)
        a = []
        for s in range(3):
            d = delayed(s, p0)
            a.append(tap(s, 0) * d[0] + tap(s, 1) * d[1] + tap(s, 2) * d[2])
            feat[s, here] = a[s]
        fields[0, here] = a[0] * a[2]
        fields[2, here] = a[1] * x[3, pl.ds(p0 + 1, chunk)]
        return carry

    lax.fori_loop(0, parts // chunk, featurize, 0)

    turn_re, turn_im = cos_ref[...], sin_ref[...]
    first, second, last = first_ref[...], second_ref[...], last_ref[...]
    flat_fields = fields.reshape(3 * width, rows)
    flat_conv = conv.reshape(3 * width, rows)

    def twiddled(re, im):
        return re * turn_re - im * turn_im, re * turn_im + im * turn_re

    def forward(f, carry):
        for c in range(0, chans, 2):
            pair = [flat_fields[pl.ds(f * width + c + e, parts, stride=chans), :] for e in (0, 1)]
            hi, lo = halves(jnp.concatenate(pair, axis=1))
            mid = jnp.dot(first, jnp.concatenate([hi, lo, hi], axis=0), preferred_element_type=F32)
            for e in (0, 1):
                re, im = twiddled(mid[:parts, e * rows : (e + 1) * rows], mid[parts:, e * rows : (e + 1) * rows])
                hi, lo = halves(jnp.concatenate([re, im], axis=1))
                lhs[(c + e) * parts : (c + e + 1) * parts, :] = jnp.concatenate([hi, lo, hi], axis=1)
        spec[f] = jnp.dot(lhs[...], second, preferred_element_type=F32)
        return carry

    lax.fori_loop(0, 3, forward, 0)

    def inverse(o, carry):
        f_a = jnp.where(o == 0, 0, 2)
        f_b = jnp.where(o == 2, 0, 1)
        sign = jnp.where(o == 0, 1.0, -1.0).astype(F32)
        for c in range(chans):
            block = pl.ds(c * parts, parts)
            a, b = spec[f_a, block, :], spec[f_b, block, :]
            a_re, a_im, b_re, b_im = a[:, :rows], a[:, rows:], b[:, :rows], sign * b[:, rows:]
            re, im = a_re * b_re - a_im * b_im, a_re * b_im + a_im * b_re
            hi, lo = halves(jnp.concatenate([re, -im], axis=1))
            lhs[c * parts : (c + 1) * parts, :] = jnp.concatenate([hi, lo, hi], axis=1)
        mid = jnp.dot(lhs[...], second, preferred_element_type=F32)
        for c in range(0, chans, 2):
            pair = []
            for e in (0, 1):
                block = mid[(c + e) * parts : (c + e + 1) * parts]
                pair.append(jnp.concatenate(twiddled(block[:, :rows], block[:, rows:]), axis=0))
            hi, lo = halves(jnp.concatenate(pair, axis=1))
            out = jnp.dot(last, jnp.concatenate([hi, lo, hi], axis=0), preferred_element_type=F32)
            for e in (0, 1):
                flat_conv[pl.ds(o * width + c + e, parts, stride=chans), :] = out[:, e * rows : (e + 1) * rows]
        return carry

    lax.fori_loop(0, 3, inverse, 0)

    def deliver(i, carry):
        sums, edge = carry
        p0 = (parts // chunk - 1 - i) * chunk
        here = pl.ds(p0, chunk)
        y, dz, dh = conv[0, here], conv[1, here], conv[2, here]
        grad = x[3, pl.ds(p0 + 1, chunk)]
        da = [dz * feat[2, here], grad * y, dz * feat[0, here]]
        mixed = feat[1, here] * y
        grads = []
        sums = list(sums)
        for s in range(3):
            value = jnp.concatenate([da[s], edge[s][None]], axis=0)
            total = tap(s, 0) * da[s]
            for j in (1, 2):
                moved = rolled(value, -j)
                total = total + tap(s, j) * jnp.where(lane >= rows - j, moved[1:], moved[:-1])
            grads.append(total)
            d = delayed(s, p0)
            for j in range(3):
                sums[3 * s + j] = sums[3 * s + j] + jnp.sum(da[s] * d[j], axis=0)
        send2[here, 0:16, :] = jnp.concatenate([mixed, grads[0]], axis=1).astype(BF16)
        send2[here, 16:32, :] = jnp.concatenate([grads[1], grads[2]], axis=1).astype(BF16)
        dh_hi = dh.astype(BF16).astype(F32)
        send2[here, 32:48, :] = jnp.concatenate([dh_hi, dh - dh_hi], axis=1).astype(BF16)
        return tuple(sums), tuple(value[0] for value in da)

    none = jnp.zeros((chans, rows), F32)
    sums, _ = lax.fori_loop(0, parts // chunk, deliver, ((none,) * 9, (none,) * 3))
    lane2 = lane[0]
    own_sums = jnp.zeros((chans, rows), F32)
    for n in range(9):
        own_sums = jnp.where(lane2 == n, jnp.sum(sums[n], axis=1, keepdims=True), own_sums)
    sums_hi = own_sums.astype(BF16).astype(F32)
    tail = jnp.concatenate([sums_hi, own_sums - sums_hi], axis=0).astype(BF16)
    send2[:, 48:64, :] = jnp.broadcast_to(tail[None], (parts, 16, rows))

    own2 = pltpu.make_async_copy(send2.at[me], recv2.at[me], recv_sem2)
    own2.start()

    def post2(peer):
        pltpu.make_async_remote_copy(
            src_ref=send2.at[peer], dst_ref=recv2.at[me], send_sem=send_sem2, recv_sem=recv_sem2, **target(peer)
        ).start()

    peers(post2)
    pltpu.make_async_copy(recv2, recv2, recv_sem2).wait()

    def back(value):
        return jnp.transpose(value.reshape(width, rows))

    pair = recv2[:, 0:16, :].astype(F32)
    mixed_ref[...] = back(pair[:, 0:8]).astype(BF16)
    gq_ref[...] = back(pair[:, 8:16]).astype(BF16)
    pair = recv2[:, 16:32, :].astype(F32)
    gk_ref[...] = back(pair[:, 0:8]).astype(BF16)
    gv_ref[...] = back(pair[:, 8:16]).astype(BF16)
    pair = recv2[:, 32:48, :].astype(F32)
    gh_ref[...] = back(pair[:, 0:8] + pair[:, 8:16])
    pair = recv2[:, 48:64, :].astype(F32)
    gtaps_ref[...] = back(pair[:, 0:8] + pair[:, 8:16])[0:9]

    sent = pl.ds(0, parts - 1)
    pltpu.make_async_copy(send.at[sent], send.at[sent], send_sem).wait()
    pltpu.make_async_copy(send2.at[sent], send2.at[sent], send_sem2).wait()


def local(q_proj, k_proj, v_proj, short_taps, long_filter, grad_out):
    parts = lax.axis_size("ctx")
    rows, width = q_proj.shape
    chans = width // parts
    tables = [jnp.asarray(t) for t in make_tables(parts, rows)]
    vmem = pl.BlockSpec(memory_space=pltpu.VMEM)
    like = jax.ShapeDtypeStruct((rows, width), BF16)
    outs = pl.pallas_call(
        kernel,
        out_shape=(
            like, like, like, like,
            jax.ShapeDtypeStruct((9, width), F32),
            jax.ShapeDtypeStruct((rows, width), F32),
        ),
        in_specs=[vmem] * 11,
        out_specs=(vmem,) * 6,
        scratch_shapes=[
            pltpu.VMEM((parts, 48, rows), BF16),
            pltpu.VMEM((parts, 48, rows), BF16),
            pltpu.VMEM((parts, 64, rows), BF16),
            pltpu.VMEM((parts, 64, rows), BF16),
            pltpu.VMEM((width, rows), F32),
            pltpu.VMEM((4, parts + 1, chans, rows), F32),
            pltpu.VMEM((3, parts, chans, rows), F32),
            pltpu.VMEM((3, parts, chans, rows), F32),
            pltpu.VMEM((3, width, 2 * rows), F32),
            pltpu.VMEM((3, parts, chans, rows), F32),
            pltpu.VMEM((width, 6 * rows), BF16),
            pltpu.SemaphoreType.DMA,
            pltpu.SemaphoreType.DMA,
            pltpu.SemaphoreType.DMA,
            pltpu.SemaphoreType.DMA,
        ],
        compiler_params=pltpu.CompilerParams(
            collective_id=0, has_side_effects=True, vmem_limit_bytes=40 << 20
        ),
        name="long_conv",
    )(q_proj, k_proj, v_proj, grad_out, long_filter, short_taps.reshape(9, width), *tables)
    mixed, gq, gk, gv, gtaps, gh = outs
    return mixed, gq, gk, gv, gtaps.reshape(3, 3, width), gh


def solution(mesh):
    field = P("ctx", "tp")
    taps = P(None, None, "tp")
    return jax.shard_map(
        local,
        mesh=mesh,
        in_specs=(field, field, field, taps, field, field),
        out_specs=(field, field, field, field, taps, field),
        check_vma=False,
    )
```

```python
import math

import jax
import jax.numpy as jnp
import numpy as np
from jax import lax
from jax.experimental import pallas as pl
from jax.experimental.pallas import tpu as pltpu
from jax.sharding import PartitionSpec as P

F32 = jnp.float32
BF16 = jnp.bfloat16
SLOTS = 16
RANGE = 32768.0
TINY = 1e-30


def encode(value):
    power = value * value
    power = power * power
    power = power * power
    return jnp.where(value < 0.0, -power, power)


def decode(coded):
    size = jnp.abs(coded)
    fourth = lax.rsqrt(lax.rsqrt(size))
    eighth = fourth * lax.rsqrt(fourth)
    return jnp.where(coded < 0.0, -eighth, jnp.where(size > 0.0, eighth, 0.0))


def split_table(table):
    hi = table.astype(BF16)
    return hi, (table - hi.astype(np.float64)).astype(BF16)


def make_tables(parts, rows):
    total = parts * rows
    k1 = np.arange(parts)
    p = np.arange(parts)
    t = np.arange(rows)
    coarse = 2.0 * math.pi * np.outer(k1 + 0.25, p) / parts
    first = np.concatenate([np.cos(coarse), -np.sin(coarse)], axis=0)
    hi, lo = split_table(first)
    first = np.concatenate([hi, hi, lo], axis=1)
    turn = 2.0 * math.pi * np.outer(k1 + 0.25, t) / total
    fine = 2.0 * math.pi * (np.outer(t, t) % rows) / rows
    second = np.block([[np.cos(fine), -np.sin(fine)], [np.sin(fine), np.cos(fine)]])
    hi, lo = split_table(second)
    second = np.concatenate([hi, hi, lo], axis=0)
    last = np.concatenate([np.cos(coarse.T), np.sin(coarse.T)], axis=1) / total
    hi, lo = split_table(last)
    last = np.concatenate([hi, hi, lo], axis=1)
    return first, second, last, np.cos(turn).astype(np.float32), -np.sin(turn).astype(np.float32)


def halves(value):
    hi = value.astype(BF16)
    return hi, (value - hi.astype(F32)).astype(BF16)


def sequence_kernel(
    q_hbm, k_hbm, v_hbm, g_hbm, h_hbm, taps_hbm, first_hbm, second_hbm, last_hbm, cos_hbm, sin_hbm,
    recv2, notes,
    send, recv, send2, notes_out, taps_t, x, feat, fields, spec, conv, lhs,
    send_sem, recv_sem, send_sem2, recv_sem2, note_send_sem, note_recv_sem,
    q_ref, k_ref, v_ref, g_ref, h_ref, taps_ref, first_ref, second_ref, last_ref, cos_ref, sin_ref, load_sem,
):
    parts, chans, rows = 64, 8, 128
    width = parts * chans
    me = lax.axis_index("ctx")
    tp = lax.axis_index("tp")
    barrier = pltpu.get_barrier_semaphore()
    loads = [
        pltpu.make_async_copy(source, held, load_sem.at[n])
        for n, (source, held) in enumerate((
            (q_hbm, q_ref), (k_hbm, k_ref), (v_hbm, v_ref), (g_hbm, g_ref), (h_hbm, h_ref), (taps_hbm, taps_ref),
            (first_hbm, first_ref), (second_hbm, second_ref), (last_hbm, last_ref), (cos_hbm, cos_ref), (sin_hbm, sin_ref),
        ))
    ]
    for load in loads:
        load.start()

    def peers(body):
        def step(i, carry):
            xi, zi = i & 3, (i >> 2) & 7
            x_off = 2 + jnp.where((xi & 1) == 1, -((xi + 1) >> 1), xi >> 1)
            z_off = 4 + jnp.where((zi & 1) == 1, -((zi + 1) >> 1), zi >> 1)
            y_off = 1 - (i >> 5)
            x_to = ((me >> 4) + x_off) & 3
            y_to = ((me >> 3) & 1) ^ y_off
            z_to = (me + z_off) & 7
            body((x_to << 4) | (y_to << 3) | z_to)
            return carry

        lax.fori_loop(0, parts - 1, step, 0)

    def target(peer):
        return dict(device_id=(peer, tp), device_id_type=pl.DeviceIdType.MESH)

    peers(lambda peer: pl.semaphore_signal(barrier, inc=1, **target(peer)))

    for load in loads[:6]:
        load.wait()

    def turned(ref):
        return jnp.transpose(ref[...].astype(F32)).reshape(parts, chans, rows)

    send[:, 0:16, :] = jnp.concatenate([turned(q_ref), turned(k_ref)], axis=1).astype(BF16)
    send[:, 16:32, :] = jnp.concatenate([turned(v_ref), turned(g_ref)], axis=1).astype(BF16)
    filt = turned(h_ref)
    filt_hi = filt.astype(BF16).astype(F32)
    send[:, 32:48, :] = jnp.concatenate([filt_hi, filt - filt_hi], axis=1).astype(BF16)
    taps = jnp.concatenate([taps_ref[0], taps_ref[1], taps_ref[2], jnp.zeros((rows - 9, width), F32)], axis=0)
    taps_t[...] = jnp.transpose(taps)

    pl.semaphore_wait(barrier, parts - 1)
    own = pltpu.make_async_copy(send.at[me], recv.at[me], recv_sem)
    own.start()

    def post(peer):
        pltpu.make_async_remote_copy(
            src_ref=send.at[peer], dst_ref=recv.at[me], send_sem=send_sem, recv_sem=recv_sem, **target(peer)
        ).start()

    peers(post)
    pltpu.make_async_copy(recv, recv, recv_sem).wait()

    own_taps = taps_t[pl.ds(pl.multiple_of(me * chans, chans), chans), :]

    def tap(s, j):
        return jnp.broadcast_to(own_taps[:, 3 * s + j : 3 * s + j + 1], (chans, rows))[None]

    lane = lax.broadcasted_iota(jnp.int32, (1, chans, rows), 2)
    chunk = 8

    def rolled(value, shift):
        flat = value.reshape(-1, rows)
        return pltpu.roll(flat, shift % rows, axis=1).reshape(value.shape)

    x[:, 0] = jnp.zeros((4, chans, rows), F32)

    def unpack(i, carry):
        p0 = i * chunk
        here = pl.ds(p0, chunk)
        there = pl.ds(p0 + 1, chunk)
        qk = recv[here, 0:16, :].astype(F32)
        vg = recv[here, 16:32, :].astype(F32)
        hh = recv[here, 32:48, :].astype(F32)
        x[0, there] = qk[:, 0:8]
        x[1, there] = qk[:, 8:16]
        x[2, there] = vg[:, 0:8]
        x[3, there] = vg[:, 8:16]
        fields[1, here] = hh[:, 0:8] + hh[:, 8:16]
        return carry

    lax.fori_loop(0, parts // chunk, unpack, 0)

    def delayed(s, p0):
        value = x[s, pl.ds(p0, chunk + 1)]
        out = [value[1:]]
        for j in (1, 2):
            moved = rolled(value, j)
            out.append(jnp.where(lane < j, moved[:-1], moved[1:]))
        return out

    def featurize(i, carry):
        p0 = i * chunk
        here = pl.ds(p0, chunk)
        a = []
        for s in range(3):
            d = delayed(s, p0)
            a.append(tap(s, 0) * d[0] + tap(s, 1) * d[1] + tap(s, 2) * d[2])
            feat[s, here] = a[s]
        fields[0, here] = a[0] * a[2]
        fields[2, here] = a[1] * x[3, pl.ds(p0 + 1, chunk)]
        return carry

    lax.fori_loop(0, parts // chunk, featurize, 0)

    for load in loads[6:]:
        load.wait()
    turn_re, turn_im = cos_ref[...], sin_ref[...]
    first, second, last = first_ref[...], second_ref[...], last_ref[...]
    flat_fields = fields.reshape(3 * width, rows)
    flat_conv = conv.reshape(3 * width, rows)

    def twiddled(re, im):
        return re * turn_re - im * turn_im, re * turn_im + im * turn_re

    def forward(f, carry):
        for c in range(0, chans, 2):
            pair = [flat_fields[pl.ds(f * width + c + e, parts, stride=chans), :] for e in (0, 1)]
            hi, lo = halves(jnp.concatenate(pair, axis=1))
            mid = jnp.dot(first, jnp.concatenate([hi, lo, hi], axis=0), preferred_element_type=F32)
            for e in (0, 1):
                re, im = twiddled(mid[:parts, e * rows : (e + 1) * rows], mid[parts:, e * rows : (e + 1) * rows])
                hi, lo = halves(jnp.concatenate([re, im], axis=1))
                lhs[(c + e) * parts : (c + e + 1) * parts, :] = jnp.concatenate([hi, lo, hi], axis=1)
        spec[f] = jnp.dot(lhs[...], second, preferred_element_type=F32)
        return carry

    lax.fori_loop(0, 3, forward, 0)

    def inverse(o, carry):
        f_a = jnp.where(o == 0, 0, 2)
        f_b = jnp.where(o == 2, 0, 1)
        sign = jnp.where(o == 0, 1.0, -1.0).astype(F32)
        for c in range(chans):
            block = pl.ds(c * parts, parts)
            a, b = spec[f_a, block, :], spec[f_b, block, :]
            a_re, a_im, b_re, b_im = a[:, :rows], a[:, rows:], b[:, :rows], sign * b[:, rows:]
            re, im = a_re * b_re - a_im * b_im, a_re * b_im + a_im * b_re
            hi, lo = halves(jnp.concatenate([re, -im], axis=1))
            lhs[c * parts : (c + 1) * parts, :] = jnp.concatenate([hi, lo, hi], axis=1)
        mid = jnp.dot(lhs[...], second, preferred_element_type=F32)
        for c in range(0, chans, 2):
            pair = []
            for e in (0, 1):
                block = mid[(c + e) * parts : (c + e + 1) * parts]
                pair.append(jnp.concatenate(twiddled(block[:, :rows], block[:, rows:]), axis=0))
            hi, lo = halves(jnp.concatenate(pair, axis=1))
            out = jnp.dot(last, jnp.concatenate([hi, lo, hi], axis=0), preferred_element_type=F32)
            for e in (0, 1):
                flat_conv[pl.ds(o * width + c + e, parts, stride=chans), :] = out[:, e * rows : (e + 1) * rows]
        return carry

    lax.fori_loop(0, 3, inverse, 0)

    peak = []
    for o in range(3):
        top = jnp.max(jnp.max(jnp.abs(conv[o]), axis=0), axis=1, keepdims=True)
        peak.append(jnp.broadcast_to(jnp.maximum(top, TINY), (chans, rows)))
    gain = [RANGE / top for top in peak]
    group = lax.broadcasted_iota(jnp.int32, (1, chans, rows), 2) // SLOTS
    sublane = lax.broadcasted_iota(jnp.int32, (1, chans, rows), 1)

    def flattened(value):
        for shift in (SLOTS, 2 * SLOTS, 4 * SLOTS):
            value = value + rolled(value, shift)
        return jnp.sum(jnp.where(group == sublane, value, 0.0), axis=1, keepdims=True)

    def placed(values, lane0):
        out = jnp.zeros_like(values[0])
        for n, value in enumerate(values):
            at = lane0 + 2 * n
            out = jnp.where((lane >= at) & (lane < at + 2), rolled(value, at) if at else value, out)
        return out

    def deliver(i, sums):
        p0 = i * chunk
        here = pl.ds(p0, chunk)
        there = pl.ds(p0 + 1, chunk)
        y, dz, dh = conv[0, here], conv[1, here], conv[2, here]
        a = [feat[s, here] for s in range(3)]
        da = [dz * a[2], x[3, there] * y, dz * a[0]]
        sums = list(sums)
        for s in range(3):
            d = delayed(s, p0)
            for j in range(3):
                sums[3 * s + j] = sums[3 * s + j] + jnp.sum(da[s] * d[j], axis=0)
        notes_out[here, 0:1, :] = flattened(placed(da, 9))
        notes_out[there, 1:2, :] = flattened(placed(a, 0))
        coded = [encode(value * gain[o][None]) for o, value in enumerate((y, dz, dh))]
        send2[here, :, :] = jnp.concatenate(coded, axis=1).astype(BF16)
        return tuple(sums)

    sums = lax.fori_loop(0, parts // chunk, deliver, (jnp.zeros((chans, rows), F32),) * 9)
    notes_out[parts, 0:1, :] = jnp.zeros((1, rows), F32)
    lane2 = lane[0]
    first_note = jnp.zeros((chans, rows), F32)
    for n in range(9):
        first_note = jnp.where(lane2 == n, jnp.sum(sums[n], axis=1, keepdims=True), first_note)
    second_note = jnp.zeros((chans, rows), F32)
    for o in range(3):
        second_note = jnp.where(lane2 == 6 + o, peak[o], second_note)
    both = jnp.concatenate([flattened(first_note[None]), flattened(second_note[None])], axis=1)
    later = pl.ds(1, parts)
    notes_out[later] = notes_out[later] + both

    own2 = pltpu.make_async_copy(send2.at[me], recv2.at[me], recv_sem2)
    own2.start()
    own_note = pltpu.make_async_copy(notes_out.at[me + 1], notes.at[me], note_recv_sem)
    own_note.start()

    def post2(peer):
        pltpu.make_async_remote_copy(
            src_ref=send2.at[peer], dst_ref=recv2.at[me], send_sem=send_sem2, recv_sem=recv_sem2, **target(peer)
        ).start()
        pltpu.make_async_remote_copy(
            src_ref=notes_out.at[peer + 1], dst_ref=notes.at[me], send_sem=note_send_sem, recv_sem=note_recv_sem, **target(peer)
        ).start()

    peers(post2)
    pltpu.make_async_copy(recv2, recv2, recv_sem2).wait()
    pltpu.make_async_copy(notes, notes, note_recv_sem).wait()
    sent = pl.ds(0, parts - 1)
    pltpu.make_async_copy(send.at[sent], send.at[sent], send_sem).wait()
    pltpu.make_async_copy(send2.at[sent], send2.at[sent], send_sem2).wait()
    pltpu.make_async_copy(notes_out.at[sent], notes_out.at[sent], note_send_sem).wait()


def home_kernel(
    q_hbm, k_hbm, v_hbm, g_hbm, taps_hbm, conv_hbm, notes_hbm,
    mixed_hbm, gq_hbm, gk_hbm, gv_hbm, gtaps_hbm, gh_hbm,
    q_ref, k_ref, v_ref, g_ref, taps_ref, conv_ref, notes_ref, load_sem,
    mixed_ref, gq_ref, gk_ref, gv_ref, gtaps_ref, gh_ref, store_sem,
    notes_t,
):
    parts, chans, rows = 64, 8, 128
    loads = [
        pltpu.make_async_copy(source, held, load_sem.at[n])
        for n, (source, held) in enumerate((
            (notes_hbm, notes_ref), (conv_hbm, conv_ref), (taps_hbm, taps_ref),
            (q_hbm, q_ref), (k_hbm, k_ref), (v_hbm, v_ref), (g_hbm, g_ref),
        ))
    ]
    for load in loads:
        load.start()
    stores = [
        pltpu.make_async_copy(held, result, store_sem.at[n])
        for n, (held, result) in enumerate((
            (gtaps_ref, gtaps_hbm), (gh_ref, gh_hbm), (mixed_ref, mixed_hbm), (gq_ref, gq_hbm), (gk_ref, gk_hbm), (gv_ref, gv_hbm),
        ))
    ]
    loads[0].wait()
    for r in range(2):
        note = notes_ref[:, r, :]
        for c in range(chans):
            notes_t[r, pl.ds(c, parts, stride=chans), :] = pltpu.roll(note, (rows - SLOTS * c) % rows, axis=1) if c else note
    for load in loads[1:]:
        load.wait()
    row = lax.broadcasted_iota(jnp.int32, (rows, rows), 0)
    inputs = (q_ref, k_ref, v_ref)
    outputs = (gq_ref, gk_ref, gv_ref)
    pad = jnp.zeros((8, rows), F32)
    for b in range(4):
        cols = slice(b * rows, (b + 1) * rows)
        groups = slice(b * 16, (b + 1) * 16)
        note = [jnp.transpose(notes_t[r, cols, :])[0:16] for r in range(2)]
        for s in range(3):
            gtaps_ref[s, :, cols] = note[0][3 * s : 3 * s + 3]
        wide = decode(conv_ref[groups].astype(F32))
        y, dz, dh = [
            jnp.transpose(wide[:, 8 * o : 8 * o + 8].reshape(rows, rows)) * (note[1][6 + o : 7 + o] * (1.0 / RANGE))
            for o in range(3)
        ]
        gh_ref[:, cols] = dh
        tap = [[taps_ref[s, j : j + 1, cols] for j in range(3)] for s in range(3)]
        a = []
        for s in range(3):
            value = inputs[s][:, cols].astype(F32)
            joined = jnp.concatenate([pad, value], axis=0)
            total = tap[s][0] * value + tap[s][1] * joined[7 : 7 + rows] + tap[s][2] * joined[6 : 6 + rows]
            total = jnp.where(row == 0, note[1][2 * s : 2 * s + 1], total)
            a.append(jnp.where(row == 1, note[1][2 * s + 1 : 2 * s + 2], total))
        mixed_ref[:, cols] = (a[1] * y).astype(BF16)
        da = [dz * a[2], g_ref[:, cols].astype(F32) * y, dz * a[0]]
        for s in range(3):
            joined = jnp.concatenate([da[s], note[0][9 + 2 * s : 11 + 2 * s], pad[0:6]], axis=0)
            total = tap[s][0] * da[s] + tap[s][1] * joined[1 : 1 + rows] + tap[s][2] * joined[2 : 2 + rows]
            outputs[s][:, cols] = total.astype(BF16)
    for store in stores:
        store.start()
    for store in stores:
        store.wait()


def local(q_proj, k_proj, v_proj, short_taps, long_filter, grad_out):
    parts = lax.axis_size("ctx")
    rows, width = q_proj.shape
    chans = width // parts
    tables = [jnp.asarray(t) for t in make_tables(parts, rows)]
    hbm = pl.BlockSpec(memory_space=pltpu.HBM)
    field = [pltpu.VMEM((rows, width), BF16) for _ in range(4)]
    wide = [pltpu.VMEM((rows, width), F32)]
    taps = [pltpu.VMEM((3, 3, width), F32)]
    conv = jax.ShapeDtypeStruct((parts, 3 * chans, rows), BF16)
    notes = jax.ShapeDtypeStruct((parts, 2, rows), F32)
    conv, notes = pl.pallas_call(
        sequence_kernel,
        out_shape=(conv, notes),
        in_specs=[hbm] * 11,
        out_specs=(hbm, hbm),
        scratch_shapes=[
            pltpu.VMEM((parts, 48, rows), BF16),
            pltpu.VMEM((parts, 48, rows), BF16),
            pltpu.VMEM((parts, 3 * chans, rows), BF16),
            pltpu.VMEM((parts + 1, 2, rows), F32),
            pltpu.VMEM((width, rows), F32),
            pltpu.VMEM((4, parts + 1, chans, rows), F32),
            pltpu.VMEM((3, parts, chans, rows), F32),
            pltpu.VMEM((3, parts, chans, rows), F32),
            pltpu.VMEM((3, width, 2 * rows), F32),
            pltpu.VMEM((3, parts, chans, rows), F32),
            pltpu.VMEM((width, 6 * rows), BF16),
            *[pltpu.SemaphoreType.DMA] * 6,
            *field,
            *wide,
            *taps,
            *[pltpu.VMEM(t.shape, t.dtype) for t in tables],
            pltpu.SemaphoreType.DMA((11,)),
        ],
        compiler_params=pltpu.CompilerParams(
            collective_id=0, has_side_effects=True, vmem_limit_bytes=63 << 20
        ),
        name="sequence_part",
    )(q_proj, k_proj, v_proj, grad_out, long_filter, short_taps, *tables)
    like = jax.ShapeDtypeStruct((rows, width), BF16)
    mixed, gq, gk, gv, gtaps, gh = pl.pallas_call(
        home_kernel,
        out_shape=(
            like, like, like, like,
            jax.ShapeDtypeStruct((3, 3, width), F32),
            jax.ShapeDtypeStruct((rows, width), F32),
        ),
        in_specs=[hbm] * 7,
        out_specs=(hbm,) * 6,
        scratch_shapes=[
            *field,
            *taps,
            pltpu.VMEM(conv.shape, conv.dtype),
            pltpu.VMEM(notes.shape, notes.dtype),
            pltpu.SemaphoreType.DMA((7,)),
            *field,
            *taps,
            *wide,
            pltpu.SemaphoreType.DMA((6,)),
            pltpu.VMEM((2, width, rows), F32),
        ],
        compiler_params=pltpu.CompilerParams(vmem_limit_bytes=63 << 20),
        name="home_part",
    )(q_proj, k_proj, v_proj, grad_out, short_taps, conv, notes)
    return mixed, gq, gk, gv, gtaps, gh


def solution(mesh):
    field = P("ctx", "tp")
    taps = P(None, None, "tp")
    return jax.shard_map(
        local,
        mesh=mesh,
        in_specs=(field, field, field, taps, field, field),
        out_specs=(field, field, field, field, taps, field),
        check_vma=False,
    )
```

```python
import math

import jax
import jax.numpy as jnp
import numpy as np
from jax import lax
from jax.experimental import pallas as pl
from jax.experimental.pallas import tpu as pltpu
from jax.sharding import PartitionSpec as P

F32 = jnp.float32
BF16 = jnp.bfloat16
SLOTS = 16
RANGE = 32768.0
TINY = 1e-30


def encode(value):
    power = value * value
    power = power * power
    power = power * power
    return jnp.where(value < 0.0, -power, power)


def decode(coded):
    size = jnp.abs(coded)
    fourth = lax.rsqrt(lax.rsqrt(size))
    eighth = fourth * lax.rsqrt(fourth)
    return jnp.where(coded < 0.0, -eighth, jnp.where(size > 0.0, eighth, 0.0))


def split_table(table):
    hi = table.astype(BF16)
    return hi, (table - hi.astype(np.float64)).astype(BF16)


def make_tables(parts, rows):
    total = parts * rows
    k1 = np.arange(parts)
    p = np.arange(parts)
    t = np.arange(rows)
    coarse = 2.0 * math.pi * np.outer(k1 + 0.25, p) / parts
    first = np.concatenate([np.cos(coarse), -np.sin(coarse)], axis=0)
    hi, lo = split_table(first)
    first = np.concatenate([hi, hi, lo], axis=1)
    turn = 2.0 * math.pi * np.outer(k1 + 0.25, t) / total
    fine = 2.0 * math.pi * (np.outer(t, t) % rows) / rows
    second = np.block([[np.cos(fine), -np.sin(fine)], [np.sin(fine), np.cos(fine)]])
    hi, lo = split_table(second)
    second = np.concatenate([hi, hi, lo], axis=0)
    last = np.concatenate([np.cos(coarse.T), np.sin(coarse.T)], axis=1) / total
    hi, lo = split_table(last)
    last = np.concatenate([hi, hi, lo], axis=1)
    return first, second, last, np.cos(turn).astype(np.float32), -np.sin(turn).astype(np.float32)


def halves(value):
    hi = value.astype(BF16)
    return hi, (value - hi.astype(F32)).astype(BF16)


def sequence_kernel(
    q_hbm, k_hbm, v_hbm, g_hbm, h_hbm, taps_hbm, first_hbm, second_hbm, last_hbm, cos_hbm, sin_hbm,
    y_in, d_in, notes,
    wave1, wave2, peaks, got1, got2, got_peaks, y_out, d_out, notes_out, taps_t, x, feat, fields, spec, conv, lhs,
    send_sem, recv_sem,
    q_ref, k_ref, v_ref, g_ref, h_ref, taps_ref, first_ref, second_ref, last_ref, cos_ref, sin_ref, load_sem,
):
    parts, chans, rows = 64, 8, 128
    width = parts * chans
    me = lax.axis_index("ctx")
    tp = lax.axis_index("tp")
    barrier = pltpu.get_barrier_semaphore()
    loads = [
        pltpu.make_async_copy(source, held, load_sem.at[n])
        for n, (source, held) in enumerate((
            (q_hbm, q_ref), (k_hbm, k_ref), (v_hbm, v_ref), (g_hbm, g_ref), (h_hbm, h_ref), (taps_hbm, taps_ref),
            (first_hbm, first_ref), (second_hbm, second_ref), (last_hbm, last_ref), (cos_hbm, cos_ref), (sin_hbm, sin_ref),
        ))
    ]

    def peers(body):
        def step(i, carry):
            xi, zi = i & 3, (i >> 2) & 7
            x_off = 2 + jnp.where((xi & 1) == 1, -((xi + 1) >> 1), xi >> 1)
            z_off = 4 + jnp.where((zi & 1) == 1, -((zi + 1) >> 1), zi >> 1)
            y_off = 1 - (i >> 5)
            x_to = ((me >> 4) + x_off) & 3
            y_to = ((me >> 3) & 1) ^ y_off
            z_to = (me + z_off) & 7
            body((x_to << 4) | (y_to << 3) | z_to)
            return carry

        lax.fori_loop(0, parts - 1, step, 0)

    def target(peer):
        return dict(device_id=(peer, tp), device_id_type=pl.DeviceIdType.MESH)

    peers(lambda peer: pl.semaphore_signal(barrier, inc=1, **target(peer)))
    for load in loads:
        load.start()

    for load in loads[:6]:
        load.wait()

    def turned(ref):
        return jnp.transpose(ref[...].astype(F32)).reshape(parts, chans, rows)

    filt = turned(h_ref)
    peak = jnp.max(jnp.max(jnp.abs(filt), axis=2, keepdims=True), axis=1, keepdims=True)
    peak = jnp.broadcast_to(jnp.maximum(peak, TINY), (parts, 1, rows))
    peaks[...] = peak
    wave1[...] = jnp.concatenate([turned(q_ref), turned(v_ref), encode(filt * (RANGE / peak))], axis=1).astype(BF16)
    wave2[...] = jnp.concatenate([turned(k_ref), turned(g_ref)], axis=1).astype(BF16)
    taps = jnp.concatenate([taps_ref[0], taps_ref[1], taps_ref[2], jnp.zeros((rows - 9, width), F32)], axis=0)
    taps_t[...] = jnp.transpose(taps)

    pl.semaphore_wait(barrier, parts - 1)

    def exchange(moves):
        for source, result, n, skip in moves:
            pltpu.make_async_copy(source.at[me + skip], result.at[me], recv_sem.at[n]).start()

        def post(peer):
            for source, result, n, skip in moves:
                pltpu.make_async_remote_copy(
                    src_ref=source.at[peer + skip], dst_ref=result.at[me],
                    send_sem=send_sem.at[n], recv_sem=recv_sem.at[n], **target(peer)
                ).start()

        peers(post)

    def arrived(result, n):
        pltpu.make_async_copy(result, result, recv_sem.at[n]).wait()

    exchange([(wave1, got1, 0, 0), (peaks, got_peaks, 1, 0)])
    exchange([(wave2, got2, 2, 0)])
    arrived(got1, 0)
    arrived(got_peaks, 1)

    own_taps = taps_t[pl.ds(pl.multiple_of(me * chans, chans), chans), :]

    def tap(s, j):
        return jnp.broadcast_to(own_taps[:, 3 * s + j : 3 * s + j + 1], (chans, rows))[None]

    lane = lax.broadcasted_iota(jnp.int32, (1, chans, rows), 2)
    chunk = 8

    def rolled(value, shift):
        flat = value.reshape(-1, rows)
        return pltpu.roll(flat, shift % rows, axis=1).reshape(value.shape)

    x[:, 0] = jnp.zeros((4, chans, rows), F32)

    def unpack1(i, carry):
        p0 = i * chunk
        here = pl.ds(p0, chunk)
        there = pl.ds(p0 + 1, chunk)
        block = got1[here].astype(F32)
        x[0, there] = block[:, 0:8]
        x[2, there] = block[:, 8:16]
        fields[1, here] = decode(block[:, 16:24]) * (got_peaks[here] * (1.0 / RANGE))
        return carry

    def unpack2(i, carry):
        p0 = i * chunk
        there = pl.ds(p0 + 1, chunk)
        block = got2[pl.ds(p0, chunk)].astype(F32)
        x[1, there] = block[:, 0:8]
        x[3, there] = block[:, 8:16]
        return carry

    lax.fori_loop(0, parts // chunk, unpack1, 0)

    def delayed(s, p0):
        value = x[s, pl.ds(p0, chunk + 1)]
        out = [value[1:]]
        for j in (1, 2):
            moved = rolled(value, j)
            out.append(jnp.where(lane < j, moved[:-1], moved[1:]))
        return out

    def featured(s, p0):
        d = delayed(s, p0)
        value = tap(s, 0) * d[0] + tap(s, 1) * d[1] + tap(s, 2) * d[2]
        feat[s, pl.ds(p0, chunk)] = value
        return value

    def featurize1(i, carry):
        p0 = i * chunk
        fields[0, pl.ds(p0, chunk)] = featured(0, p0) * featured(2, p0)
        return carry

    def featurize2(i, carry):
        p0 = i * chunk
        fields[2, pl.ds(p0, chunk)] = featured(1, p0) * x[3, pl.ds(p0 + 1, chunk)]
        return carry

    lax.fori_loop(0, parts // chunk, featurize1, 0)

    for load in loads[6:]:
        load.wait()
    turn_re, turn_im = cos_ref[...], sin_ref[...]
    first, second, last = first_ref[...], second_ref[...], last_ref[...]
    flat_fields = fields.reshape(3 * width, rows)
    flat_conv = conv.reshape(3 * width, rows)

    def twiddled(re, im):
        return re * turn_re - im * turn_im, re * turn_im + im * turn_re

    def forward(f, carry):
        for c in range(0, chans, 2):
            pair = [flat_fields[pl.ds(f * width + c + e, parts, stride=chans), :] for e in (0, 1)]
            hi, lo = halves(jnp.concatenate(pair, axis=1))
            mid = jnp.dot(first, jnp.concatenate([hi, lo, hi], axis=0), preferred_element_type=F32)
            for e in (0, 1):
                re, im = twiddled(mid[:parts, e * rows : (e + 1) * rows], mid[parts:, e * rows : (e + 1) * rows])
                hi, lo = halves(jnp.concatenate([re, im], axis=1))
                lhs[(c + e) * parts : (c + e + 1) * parts, :] = jnp.concatenate([hi, lo, hi], axis=1)
        spec[f] = jnp.dot(lhs[...], second, preferred_element_type=F32)
        return carry

    lax.fori_loop(0, 2, forward, 0)

    def inverse(o, carry):
        f_a = jnp.where(o == 0, 0, 2)
        f_b = jnp.where(o == 2, 0, 1)
        sign = jnp.where(o == 0, 1.0, -1.0).astype(F32)
        for c in range(chans):
            block = pl.ds(c * parts, parts)
            a, b = spec[f_a, block, :], spec[f_b, block, :]
            a_re, a_im, b_re, b_im = a[:, :rows], a[:, rows:], b[:, :rows], sign * b[:, rows:]
            re, im = a_re * b_re - a_im * b_im, a_re * b_im + a_im * b_re
            hi, lo = halves(jnp.concatenate([re, -im], axis=1))
            lhs[c * parts : (c + 1) * parts, :] = jnp.concatenate([hi, lo, hi], axis=1)
        mid = jnp.dot(lhs[...], second, preferred_element_type=F32)
        for c in range(0, chans, 2):
            pair = []
            for e in (0, 1):
                block = mid[(c + e) * parts : (c + e + 1) * parts]
                pair.append(jnp.concatenate(twiddled(block[:, :rows], block[:, rows:]), axis=0))
            hi, lo = halves(jnp.concatenate(pair, axis=1))
            out = jnp.dot(last, jnp.concatenate([hi, lo, hi], axis=0), preferred_element_type=F32)
            for e in (0, 1):
                flat_conv[pl.ds(o * width + c + e, parts, stride=chans), :] = out[:, e * rows : (e + 1) * rows]
        return carry

    def scaled(o):
        top = jnp.max(jnp.max(jnp.abs(conv[o]), axis=0), axis=1, keepdims=True)
        top = jnp.broadcast_to(jnp.maximum(top, TINY), (chans, rows))
        return top, (RANGE / top)[None]

    lax.fori_loop(0, 1, inverse, 0)
    y_peak, y_gain = scaled(0)

    def code_y(i, carry):
        here = pl.ds(i * chunk, chunk)
        y_out[here] = encode(conv[0, here] * y_gain).astype(BF16)
        return carry

    lax.fori_loop(0, parts // chunk, code_y, 0)
    exchange([(y_out, y_in, 3, 0)])

    arrived(got2, 2)
    lax.fori_loop(0, parts // chunk, unpack2, 0)
    lax.fori_loop(0, parts // chunk, featurize2, 0)
    lax.fori_loop(2, 3, forward, 0)
    lax.fori_loop(1, 3, inverse, 0)
    dz_peak, dz_gain = scaled(1)
    dh_peak, dh_gain = scaled(2)
    peak = (y_peak, dz_peak, dh_peak)
    group = lax.broadcasted_iota(jnp.int32, (1, chans, rows), 2) // SLOTS
    sublane = lax.broadcasted_iota(jnp.int32, (1, chans, rows), 1)

    def flattened(value):
        for shift in (SLOTS, 2 * SLOTS, 4 * SLOTS):
            value = value + rolled(value, shift)
        return jnp.sum(jnp.where(group == sublane, value, 0.0), axis=1, keepdims=True)

    def placed(values, lane0):
        out = jnp.zeros_like(values[0])
        for n, value in enumerate(values):
            at = lane0 + 2 * n
            out = jnp.where((lane >= at) & (lane < at + 2), rolled(value, at) if at else value, out)
        return out

    def deliver(i, sums):
        p0 = i * chunk
        here = pl.ds(p0, chunk)
        there = pl.ds(p0 + 1, chunk)
        y, dz, dh = conv[0, here], conv[1, here], conv[2, here]
        a = [feat[s, here] for s in range(3)]
        da = [dz * a[2], x[3, there] * y, dz * a[0]]
        sums = list(sums)
        for s in range(3):
            d = delayed(s, p0)
            for j in range(3):
                sums[3 * s + j] = sums[3 * s + j] + jnp.sum(da[s] * d[j], axis=0)
        notes_out[here, 0:1, :] = flattened(placed(da, 9))
        notes_out[there, 1:2, :] = flattened(placed(a, 0))
        d_out[here] = jnp.concatenate([encode(dz * dz_gain), encode(dh * dh_gain)], axis=1).astype(BF16)
        return tuple(sums)

    sums = lax.fori_loop(0, parts // chunk, deliver, (jnp.zeros((chans, rows), F32),) * 9)
    notes_out[parts, 0:1, :] = jnp.zeros((1, rows), F32)
    lane2 = lane[0]
    first_note = jnp.zeros((chans, rows), F32)
    for n in range(9):
        first_note = jnp.where(lane2 == n, jnp.sum(sums[n], axis=1, keepdims=True), first_note)
    second_note = jnp.zeros((chans, rows), F32)
    for o in range(3):
        second_note = jnp.where(lane2 == 6 + o, peak[o], second_note)
    both = jnp.concatenate([flattened(first_note[None]), flattened(second_note[None])], axis=1)
    later = pl.ds(1, parts)
    notes_out[later] = notes_out[later] + both

    exchange([(d_out, d_in, 4, 0), (notes_out, notes, 5, 1)])
    arrived(y_in, 3)
    arrived(d_in, 4)
    arrived(notes, 5)
    for n, source in enumerate((wave1, peaks, wave2, y_out, d_out, notes_out)):
        sent = source.at[pl.ds(0, parts - 1)]
        pltpu.make_async_copy(sent, sent, send_sem.at[n]).wait()


def home_kernel(
    q_hbm, k_hbm, v_hbm, g_hbm, taps_hbm, y_hbm, d_hbm, notes_hbm,
    mixed_hbm, gq_hbm, gk_hbm, gv_hbm, gtaps_hbm, gh_hbm,
    q_ref, k_ref, v_ref, g_ref, taps_ref, y_ref, d_ref, notes_ref, load_sem,
    mixed_ref, gq_ref, gk_ref, gv_ref, gtaps_ref, gh_ref, store_sem,
    notes_t,
):
    parts, chans, rows = 64, 8, 128
    loads = [
        pltpu.make_async_copy(source, held, load_sem.at[n])
        for n, (source, held) in enumerate((
            (notes_hbm, notes_ref), (y_hbm, y_ref), (d_hbm, d_ref), (taps_hbm, taps_ref),
            (q_hbm, q_ref), (k_hbm, k_ref), (v_hbm, v_ref), (g_hbm, g_ref),
        ))
    ]
    for load in loads:
        load.start()
    stores = [
        pltpu.make_async_copy(held, result, store_sem.at[n])
        for n, (held, result) in enumerate((
            (gtaps_ref, gtaps_hbm), (gh_ref, gh_hbm), (mixed_ref, mixed_hbm), (gq_ref, gq_hbm), (gk_ref, gk_hbm), (gv_ref, gv_hbm),
        ))
    ]
    loads[0].wait()
    for r in range(2):
        note = notes_ref[:, r, :]
        for c in range(chans):
            notes_t[r, pl.ds(c, parts, stride=chans), :] = pltpu.roll(note, (rows - SLOTS * c) % rows, axis=1) if c else note
    for load in loads[1:]:
        load.wait()
    row = lax.broadcasted_iota(jnp.int32, (rows, rows), 0)
    inputs = (q_ref, k_ref, v_ref)
    outputs = (gq_ref, gk_ref, gv_ref)
    pad = jnp.zeros((8, rows), F32)
    for b in range(4):
        cols = slice(b * rows, (b + 1) * rows)
        groups = slice(b * 16, (b + 1) * 16)
        note = [jnp.transpose(notes_t[r, cols, :])[0:16] for r in range(2)]
        for s in range(3):
            gtaps_ref[s, :, cols] = note[0][3 * s : 3 * s + 3]
        pair = decode(d_ref[groups].astype(F32))
        y, dz, dh = [
            jnp.transpose(value.reshape(rows, rows)) * (note[1][6 + o : 7 + o] * (1.0 / RANGE))
            for o, value in enumerate((decode(y_ref[groups].astype(F32)), pair[:, 0:8], pair[:, 8:16]))
        ]
        gh_ref[:, cols] = dh
        tap = [[taps_ref[s, j : j + 1, cols] for j in range(3)] for s in range(3)]
        a = []
        for s in range(3):
            value = inputs[s][:, cols].astype(F32)
            joined = jnp.concatenate([pad, value], axis=0)
            total = tap[s][0] * value + tap[s][1] * joined[7 : 7 + rows] + tap[s][2] * joined[6 : 6 + rows]
            total = jnp.where(row == 0, note[1][2 * s : 2 * s + 1], total)
            a.append(jnp.where(row == 1, note[1][2 * s + 1 : 2 * s + 2], total))
        mixed_ref[:, cols] = (a[1] * y).astype(BF16)
        da = [dz * a[2], g_ref[:, cols].astype(F32) * y, dz * a[0]]
        for s in range(3):
            joined = jnp.concatenate([da[s], note[0][9 + 2 * s : 11 + 2 * s], pad[0:6]], axis=0)
            total = tap[s][0] * da[s] + tap[s][1] * joined[1 : 1 + rows] + tap[s][2] * joined[2 : 2 + rows]
            outputs[s][:, cols] = total.astype(BF16)
    for store in stores:
        store.start()
    for store in stores:
        store.wait()


def local(q_proj, k_proj, v_proj, short_taps, long_filter, grad_out):
    parts = lax.axis_size("ctx")
    rows, width = q_proj.shape
    chans = width // parts
    tables = [jnp.asarray(t) for t in make_tables(parts, rows)]
    hbm = pl.BlockSpec(memory_space=pltpu.HBM)
    field = [pltpu.VMEM((rows, width), BF16) for _ in range(4)]
    wide = [pltpu.VMEM((rows, width), F32)]
    taps = [pltpu.VMEM((3, 3, width), F32)]
    y_all = jax.ShapeDtypeStruct((parts, chans, rows), BF16)
    d_all = jax.ShapeDtypeStruct((parts, 2 * chans, rows), BF16)
    notes = jax.ShapeDtypeStruct((parts, 2, rows), F32)
    back = pl.pallas_call(
        sequence_kernel,
        out_shape=(y_all, d_all, notes),
        in_specs=[hbm] * 11,
        out_specs=(hbm,) * 3,
        scratch_shapes=[
            *[
                pltpu.VMEM((parts, 3 * chans, rows), BF16),
                pltpu.VMEM((parts, 2 * chans, rows), BF16),
                pltpu.VMEM((parts, 1, rows), F32),
            ] * 2,
            pltpu.VMEM(y_all.shape, BF16),
            pltpu.VMEM(d_all.shape, BF16),
            pltpu.VMEM((parts + 1, 2, rows), F32),
            pltpu.VMEM((width, rows), F32),
            pltpu.VMEM((4, parts + 1, chans, rows), F32),
            pltpu.VMEM((3, parts, chans, rows), F32),
            pltpu.VMEM((3, parts, chans, rows), F32),
            pltpu.VMEM((3, width, 2 * rows), F32),
            pltpu.VMEM((3, parts, chans, rows), F32),
            pltpu.VMEM((width, 6 * rows), BF16),
            *[pltpu.SemaphoreType.DMA((6,))] * 2,
            *field,
            *wide,
            *taps,
            *[pltpu.VMEM(t.shape, t.dtype) for t in tables],
            pltpu.SemaphoreType.DMA((11,)),
        ],
        compiler_params=pltpu.CompilerParams(
            collective_id=0, has_side_effects=True, vmem_limit_bytes=63 << 20
        ),
        name="sequence_part",
    )(q_proj, k_proj, v_proj, grad_out, long_filter, short_taps, *tables)
    like = jax.ShapeDtypeStruct((rows, width), BF16)
    mixed, gq, gk, gv, gtaps, gh = pl.pallas_call(
        home_kernel,
        out_shape=(
            like, like, like, like,
            jax.ShapeDtypeStruct((3, 3, width), F32),
            jax.ShapeDtypeStruct((rows, width), F32),
        ),
        in_specs=[hbm] * 8,
        out_specs=(hbm,) * 6,
        scratch_shapes=[
            *field,
            *taps,
            *[pltpu.VMEM(value.shape, value.dtype) for value in back],
            pltpu.SemaphoreType.DMA((8,)),
            *field,
            *taps,
            *wide,
            pltpu.SemaphoreType.DMA((6,)),
            pltpu.VMEM((2, width, rows), F32),
        ],
        compiler_params=pltpu.CompilerParams(vmem_limit_bytes=63 << 20),
        name="home_part",
    )(q_proj, k_proj, v_proj, grad_out, short_taps, *back)
    return mixed, gq, gk, gv, gtaps, gh


def solution(mesh):
    field = P("ctx", "tp")
    taps = P(None, None, "tp")
    return jax.shard_map(
        local,
        mesh=mesh,
        in_specs=(field, field, field, taps, field, field),
        out_specs=(field, field, field, field, taps, field),
        check_vma=False,
    )
```

```python
import math

import jax
import jax.numpy as jnp
import numpy as np
from jax import lax
from jax.experimental import pallas as pl
from jax.experimental.pallas import tpu as pltpu
from jax.sharding import PartitionSpec as P

F32 = jnp.float32
BF16 = jnp.bfloat16
SLOTS = 16
RANGE = 32768.0
TINY = 1e-30


def encode(value):
    power = value * value
    power = power * power
    power = power * power
    return jnp.where(value < 0.0, -power, power)


def decode(coded):
    size = jnp.abs(coded)
    fourth = lax.rsqrt(lax.rsqrt(size))
    eighth = fourth * lax.rsqrt(fourth)
    return jnp.where(coded < 0.0, -eighth, jnp.where(size > 0.0, eighth, 0.0))


def split_table(table):
    hi = table.astype(BF16)
    return hi, (table - hi.astype(np.float64)).astype(BF16)


def make_tables(parts, rows):
    total = parts * rows
    k1 = np.arange(parts)
    p = np.arange(parts)
    t = np.arange(rows)
    coarse = 2.0 * math.pi * np.outer(k1 + 0.25, p) / parts
    first = np.concatenate([np.cos(coarse), -np.sin(coarse)], axis=0)
    hi, lo = split_table(first)
    first = np.concatenate([hi, hi, lo], axis=1)
    turn = 2.0 * math.pi * np.outer(k1 + 0.25, t) / total
    fine = 2.0 * math.pi * (np.outer(t, t) % rows) / rows
    second = np.block([[np.cos(fine), -np.sin(fine)], [np.sin(fine), np.cos(fine)]])
    hi, lo = split_table(second)
    second = np.concatenate([hi, hi, lo], axis=0)
    last = np.concatenate([np.cos(coarse.T), np.sin(coarse.T)], axis=1) / total
    hi, lo = split_table(last)
    last = np.concatenate([hi, hi, lo], axis=1)
    return first, second, last, np.cos(turn).astype(np.float32), -np.sin(turn).astype(np.float32)


def halves(value):
    hi = value.astype(BF16)
    return hi, (value - hi.astype(F32)).astype(BF16)


def sequence_kernel(
    q_hbm, k_hbm, v_hbm, g_hbm, h_hbm, taps_hbm, first_hbm, second_hbm, last_hbm, cos_hbm, sin_hbm,
    y_in, d_in, notes,
    wave1, wave2, peaks, got1, got2, got_peaks, y_out, d_out, notes_out, taps_t, x, late, feat, fields, spec, conv, lhs,
    send_sem, recv_sem,
    q_ref, k_ref, v_ref, g_ref, h_ref, taps_ref, first_ref, second_ref, last_ref, cos_ref, sin_ref, load_sem,
):
    parts, chans, rows = 64, 8, 128
    width = parts * chans
    me = lax.axis_index("ctx")
    tp = lax.axis_index("tp")
    barrier = pltpu.get_barrier_semaphore()
    loads = [
        pltpu.make_async_copy(source, held, load_sem.at[n])
        for n, (source, held) in enumerate((
            (q_hbm, q_ref), (k_hbm, k_ref), (v_hbm, v_ref), (g_hbm, g_ref), (h_hbm, h_ref), (taps_hbm, taps_ref),
            (first_hbm, first_ref), (second_hbm, second_ref), (last_hbm, last_ref), (cos_hbm, cos_ref), (sin_hbm, sin_ref),
        ))
    ]

    def peers(body):
        def step(i, carry):
            xi, zi = (i >> 1) & 3, i >> 3
            x_off = 2 + jnp.where((xi & 1) == 1, -((xi + 1) >> 1), xi >> 1)
            z_off = 4 + jnp.where((zi & 1) == 1, -((zi + 1) >> 1), zi >> 1)
            y_off = 1 - (i & 1)
            x_to = ((me >> 4) + x_off) & 3
            y_to = ((me >> 3) & 1) ^ y_off
            z_to = (me + z_off) & 7
            body((x_to << 4) | (y_to << 3) | z_to)
            return carry

        lax.fori_loop(0, parts - 1, step, 0)

    def target(peer):
        return dict(device_id=(peer, tp), device_id_type=pl.DeviceIdType.MESH)

    peers(lambda peer: pl.semaphore_signal(barrier, inc=1, **target(peer)))
    for load in loads:
        load.start()

    for load in loads[:6]:
        load.wait()

    def turned(ref):
        return jnp.transpose(ref[...].astype(F32)).reshape(parts, chans, rows)

    filt = turned(h_ref)
    peak = jnp.max(jnp.max(jnp.abs(filt), axis=2, keepdims=True), axis=1, keepdims=True)
    peak = jnp.broadcast_to(jnp.maximum(peak, TINY), (parts, 1, rows))
    peaks[...] = peak
    wave1[...] = jnp.concatenate([turned(q_ref), turned(v_ref), encode(filt * (RANGE / peak))], axis=1).astype(BF16)
    wave2[...] = jnp.concatenate([turned(k_ref), turned(g_ref)], axis=1).astype(BF16)
    taps = jnp.concatenate([taps_ref[0], taps_ref[1], taps_ref[2], jnp.zeros((rows - 9, width), F32)], axis=0)
    taps_t[...] = jnp.transpose(taps)

    pl.semaphore_wait(barrier, parts - 1)

    def exchange(moves):
        for source, result, n, skip in moves:
            pltpu.make_async_copy(source.at[me + skip], result.at[me], recv_sem.at[n]).start()

        def post(peer):
            for source, result, n, skip in moves:
                pltpu.make_async_remote_copy(
                    src_ref=source.at[peer + skip], dst_ref=result.at[me],
                    send_sem=send_sem.at[n], recv_sem=recv_sem.at[n], **target(peer)
                ).start()

        peers(post)

    def arrived(result, n):
        pltpu.make_async_copy(result, result, recv_sem.at[n]).wait()

    exchange([(wave1, got1, 0, 0), (peaks, got_peaks, 1, 0)])
    exchange([(wave2, got2, 2, 0)])
    arrived(got1, 0)
    arrived(got_peaks, 1)

    own_taps = taps_t[pl.ds(pl.multiple_of(me * chans, chans), chans), :]

    def tap(s, j):
        return jnp.broadcast_to(own_taps[:, 3 * s + j : 3 * s + j + 1], (chans, rows))[None]

    lane = lax.broadcasted_iota(jnp.int32, (1, chans, rows), 2)
    chunk = 8

    def rolled(value, shift):
        flat = value.reshape(-1, rows)
        return pltpu.roll(flat, shift % rows, axis=1).reshape(value.shape)

    x[:, 0] = jnp.zeros((4, chans, rows), F32)

    def unpack1(i, carry):
        p0 = i * chunk
        here = pl.ds(p0, chunk)
        there = pl.ds(p0 + 1, chunk)
        block = got1[here].astype(F32)
        x[0, there] = block[:, 0:8]
        x[2, there] = block[:, 8:16]
        fields[1, here] = decode(block[:, 16:24]) * (got_peaks[here] * (1.0 / RANGE))
        return carry

    def unpack2(i, carry):
        p0 = i * chunk
        there = pl.ds(p0 + 1, chunk)
        block = got2[pl.ds(p0, chunk)].astype(F32)
        x[1, there] = block[:, 0:8]
        x[3, there] = block[:, 8:16]
        return carry

    lax.fori_loop(0, parts // chunk, unpack1, 0, unroll=True)

    def delayed(s, p0):
        value = x[s, pl.ds(p0, chunk + 1)]
        out = [value[1:]]
        for j in (1, 2):
            moved = rolled(value, j)
            out.append(jnp.where(lane < j, moved[:-1], moved[1:]))
        return out

    def featured(s, p0):
        d = delayed(s, p0)
        here = pl.ds(p0, chunk)
        late[s, 0, here] = d[1]
        late[s, 1, here] = d[2]
        value = tap(s, 0) * d[0] + tap(s, 1) * d[1] + tap(s, 2) * d[2]
        feat[s, here] = value
        return value

    def featurize1(i, carry):
        p0 = i * chunk
        fields[0, pl.ds(p0, chunk)] = featured(0, p0) * featured(2, p0)
        return carry

    def featurize2(i, carry):
        p0 = i * chunk
        fields[2, pl.ds(p0, chunk)] = featured(1, p0) * x[3, pl.ds(p0 + 1, chunk)]
        return carry

    lax.fori_loop(0, parts // chunk, featurize1, 0, unroll=True)

    for load in loads[6:]:
        load.wait()
    turn_re, turn_im = cos_ref[...], sin_ref[...]
    first, second, last = first_ref[...], second_ref[...], last_ref[...]
    flat_fields = fields.reshape(3 * width, rows)
    flat_conv = conv.reshape(3 * width, rows)

    def twiddled(re, im):
        return re * turn_re - im * turn_im, re * turn_im + im * turn_re

    def forward(f):
        for c in range(0, chans, 2):
            pair = [flat_fields[pl.ds(f * width + c + e, parts, stride=chans), :] for e in (0, 1)]
            hi, lo = halves(jnp.concatenate(pair, axis=1))
            mid = jnp.dot(first, jnp.concatenate([hi, lo, hi], axis=0), preferred_element_type=F32)
            for e in (0, 1):
                re, im = twiddled(mid[:parts, e * rows : (e + 1) * rows], mid[parts:, e * rows : (e + 1) * rows])
                hi, lo = halves(jnp.concatenate([re, im], axis=1))
                lhs[f, (c + e) * parts : (c + e + 1) * parts, :] = jnp.concatenate([hi, lo, hi], axis=1)
        spec[f] = jnp.dot(lhs[f], second, preferred_element_type=F32)

    forward(0)
    forward(1)

    def inverse(o):
        f_a, f_b, sign = ((0, 1, 1.0), (2, 1, -1.0), (2, 0, -1.0))[o]
        for c in range(chans):
            block = pl.ds(c * parts, parts)
            a, b = spec[f_a, block, :], spec[f_b, block, :]
            a_re, a_im, b_re, b_im = a[:, :rows], a[:, rows:], b[:, :rows], sign * b[:, rows:]
            re, im = a_re * b_re - a_im * b_im, a_re * b_im + a_im * b_re
            hi, lo = halves(jnp.concatenate([re, -im], axis=1))
            lhs[o, c * parts : (c + 1) * parts, :] = jnp.concatenate([hi, lo, hi], axis=1)
        mid = jnp.dot(lhs[o], second, preferred_element_type=F32)
        for c in range(0, chans, 2):
            pair = []
            for e in (0, 1):
                block = mid[(c + e) * parts : (c + e + 1) * parts]
                pair.append(jnp.concatenate(twiddled(block[:, :rows], block[:, rows:]), axis=0))
            hi, lo = halves(jnp.concatenate(pair, axis=1))
            out = jnp.dot(last, jnp.concatenate([hi, lo, hi], axis=0), preferred_element_type=F32)
            for e in (0, 1):
                flat_conv[pl.ds(o * width + c + e, parts, stride=chans), :] = out[:, e * rows : (e + 1) * rows]

    def scaled(o):
        top = jnp.max(jnp.max(jnp.abs(conv[o]), axis=0), axis=1, keepdims=True)
        top = jnp.broadcast_to(jnp.maximum(top, TINY), (chans, rows))
        return top, (RANGE / top)[None]

    inverse(0)
    y_peak, y_gain = scaled(0)

    def code_y(i, carry):
        here = pl.ds(i * chunk, chunk)
        y_out[here] = encode(conv[0, here] * y_gain).astype(BF16)
        return carry

    lax.fori_loop(0, parts // chunk, code_y, 0, unroll=True)
    exchange([(y_out, y_in, 3, 0)])

    arrived(got2, 2)
    lax.fori_loop(0, parts // chunk, unpack2, 0, unroll=True)
    lax.fori_loop(0, parts // chunk, featurize2, 0, unroll=True)
    forward(2)
    inverse(1)
    inverse(2)
    dz_peak, dz_gain = scaled(1)
    dh_peak, dh_gain = scaled(2)
    peak = (y_peak, dz_peak, dh_peak)

    def code_d(i, carry):
        here = pl.ds(i * chunk, chunk)
        pair = [encode(conv[1, here] * dz_gain), encode(conv[2, here] * dh_gain)]
        d_out[here] = jnp.concatenate(pair, axis=1).astype(BF16)
        return carry

    lax.fori_loop(0, parts // chunk, code_d, 0, unroll=True)
    exchange([(d_out, d_in, 4, 0)])

    group = lax.broadcasted_iota(jnp.int32, (1, chans, rows), 2) // SLOTS
    sublane = lax.broadcasted_iota(jnp.int32, (1, chans, rows), 1)

    def flattened(value):
        for shift in (SLOTS, 2 * SLOTS, 4 * SLOTS):
            value = value + rolled(value, shift)
        return jnp.sum(jnp.where(group == sublane, value, 0.0), axis=1, keepdims=True)

    def placed(values, lane0):
        out = jnp.zeros_like(values[0])
        for n, value in enumerate(values):
            at = lane0 + 2 * n
            out = jnp.where((lane >= at) & (lane < at + 2), rolled(value, at) if at else value, out)
        return out

    def tally(i, sums):
        p0 = i * chunk
        here = pl.ds(p0, chunk)
        there = pl.ds(p0 + 1, chunk)
        y, dz = conv[0, here], conv[1, here]
        a = [feat[s, here] for s in range(3)]
        da = [dz * a[2], x[3, there] * y, dz * a[0]]
        sums = list(sums)
        for s in range(3):
            d = (x[s, there], late[s, 0, here], late[s, 1, here])
            for j in range(3):
                sums[3 * s + j] = sums[3 * s + j] + jnp.sum(da[s] * d[j], axis=0)
        notes_out[here, 0:1, :] = flattened(placed(da, 9))
        notes_out[there, 1:2, :] = flattened(placed(a, 0))
        return tuple(sums)

    sums = lax.fori_loop(0, parts // chunk, tally, (jnp.zeros((chans, rows), F32),) * 9, unroll=2)
    notes_out[parts, 0:1, :] = jnp.zeros((1, rows), F32)
    lane2 = lane[0]
    first_note = jnp.zeros((chans, rows), F32)
    for n in range(9):
        first_note = jnp.where(lane2 == n, jnp.sum(sums[n], axis=1, keepdims=True), first_note)
    second_note = jnp.zeros((chans, rows), F32)
    for o in range(3):
        second_note = jnp.where(lane2 == 6 + o, peak[o], second_note)
    both = jnp.concatenate([flattened(first_note[None]), flattened(second_note[None])], axis=1)
    later = pl.ds(1, parts)
    notes_out[later] = notes_out[later] + both

    exchange([(notes_out, notes, 5, 1)])
    arrived(y_in, 3)
    arrived(d_in, 4)
    arrived(notes, 5)
    for n, source in enumerate((wave1, peaks, wave2, y_out, d_out, notes_out)):
        sent = source.at[pl.ds(0, parts - 1)]
        pltpu.make_async_copy(sent, sent, send_sem.at[n]).wait()


def home_kernel(
    q_hbm, k_hbm, v_hbm, g_hbm, taps_hbm, y_hbm, d_hbm, notes_hbm,
    mixed_hbm, gq_hbm, gk_hbm, gv_hbm, gtaps_hbm, gh_hbm,
    q_ref, k_ref, v_ref, g_ref, taps_ref, y_ref, d_ref, notes_ref, load_sem,
    mixed_ref, gq_ref, gk_ref, gv_ref, gtaps_ref, gh_ref, store_sem,
    notes_t,
):
    parts, chans, rows = 64, 8, 128
    loads = [
        pltpu.make_async_copy(source, held, load_sem.at[n])
        for n, (source, held) in enumerate((
            (notes_hbm, notes_ref), (y_hbm, y_ref), (d_hbm, d_ref), (taps_hbm, taps_ref),
            (q_hbm, q_ref), (k_hbm, k_ref), (v_hbm, v_ref), (g_hbm, g_ref),
        ))
    ]
    for load in loads:
        load.start()
    results = (
        (gtaps_ref, gtaps_hbm), (gh_ref, gh_hbm), (mixed_ref, mixed_hbm), (gq_ref, gq_hbm), (gk_ref, gk_hbm), (gv_ref, gv_hbm),
    )
    stores = []
    loads[0].wait()
    for r in range(2):
        note = notes_ref[:, r, :]
        for c in range(chans):
            notes_t[r, pl.ds(c, parts, stride=chans), :] = pltpu.roll(note, (rows - SLOTS * c) % rows, axis=1) if c else note
    for load in loads[1:]:
        load.wait()
    row = lax.broadcasted_iota(jnp.int32, (rows, rows), 0)
    inputs = (q_ref, k_ref, v_ref)
    outputs = (gq_ref, gk_ref, gv_ref)
    pad = jnp.zeros((8, rows), F32)
    for b in range(4):
        cols = slice(b * rows, (b + 1) * rows)
        groups = slice(b * 16, (b + 1) * 16)
        note = [jnp.transpose(notes_t[r, cols, :])[0:16] for r in range(2)]
        for s in range(3):
            gtaps_ref[s, :, cols] = note[0][3 * s : 3 * s + 3]
        pair = decode(d_ref[groups].astype(F32))
        y, dz, dh = [
            jnp.transpose(value.reshape(rows, rows)) * (note[1][6 + o : 7 + o] * (1.0 / RANGE))
            for o, value in enumerate((decode(y_ref[groups].astype(F32)), pair[:, 0:8], pair[:, 8:16]))
        ]
        gh_ref[:, cols] = dh
        tap = [[taps_ref[s, j : j + 1, cols] for j in range(3)] for s in range(3)]
        a = []
        for s in range(3):
            value = inputs[s][:, cols].astype(F32)
            joined = jnp.concatenate([pad, value], axis=0)
            total = tap[s][0] * value + tap[s][1] * joined[7 : 7 + rows] + tap[s][2] * joined[6 : 6 + rows]
            total = jnp.where(row == 0, note[1][2 * s : 2 * s + 1], total)
            a.append(jnp.where(row == 1, note[1][2 * s + 1 : 2 * s + 2], total))
        mixed_ref[:, cols] = (a[1] * y).astype(BF16)
        da = [dz * a[2], g_ref[:, cols].astype(F32) * y, dz * a[0]]
        for s in range(3):
            joined = jnp.concatenate([da[s], note[0][9 + 2 * s : 11 + 2 * s], pad[0:6]], axis=0)
            total = tap[s][0] * da[s] + tap[s][1] * joined[1 : 1 + rows] + tap[s][2] * joined[2 : 2 + rows]
            outputs[s][:, cols] = total.astype(BF16)
        for n, (held, result) in enumerate(results):
            block = (slice(None),) * (len(held.shape) - 1) + (cols,)
            store = pltpu.make_async_copy(held.at[block], result.at[block], store_sem.at[b, n])
            store.start()
            stores.append(store)
    for store in stores:
        store.wait()


def local(q_proj, k_proj, v_proj, short_taps, long_filter, grad_out):
    parts = lax.axis_size("ctx")
    rows, width = q_proj.shape
    chans = width // parts
    tables = [jnp.asarray(t) for t in make_tables(parts, rows)]
    hbm = pl.BlockSpec(memory_space=pltpu.HBM)
    field = [pltpu.VMEM((rows, width), BF16) for _ in range(4)]
    wide = [pltpu.VMEM((rows, width), F32)]
    taps = [pltpu.VMEM((3, 3, width), F32)]
    y_all = jax.ShapeDtypeStruct((parts, chans, rows), BF16)
    d_all = jax.ShapeDtypeStruct((parts, 2 * chans, rows), BF16)
    notes = jax.ShapeDtypeStruct((parts, 2, rows), F32)
    back = pl.pallas_call(
        sequence_kernel,
        out_shape=(y_all, d_all, notes),
        in_specs=[hbm] * 11,
        out_specs=(hbm,) * 3,
        scratch_shapes=[
            *[
                pltpu.VMEM((parts, 3 * chans, rows), BF16),
                pltpu.VMEM((parts, 2 * chans, rows), BF16),
                pltpu.VMEM((parts, 1, rows), F32),
            ] * 2,
            pltpu.VMEM(y_all.shape, BF16),
            pltpu.VMEM(d_all.shape, BF16),
            pltpu.VMEM((parts + 1, 2, rows), F32),
            pltpu.VMEM((width, rows), F32),
            pltpu.VMEM((4, parts + 1, chans, rows), F32),
            pltpu.VMEM((3, 2, parts, chans, rows), F32),
            pltpu.VMEM((3, parts, chans, rows), F32),
            pltpu.VMEM((3, parts, chans, rows), F32),
            pltpu.VMEM((3, width, 2 * rows), F32),
            pltpu.VMEM((3, parts, chans, rows), F32),
            pltpu.VMEM((3, width, 6 * rows), BF16),
            *[pltpu.SemaphoreType.DMA((6,))] * 2,
            *field,
            *wide,
            *taps,
            *[pltpu.VMEM(t.shape, t.dtype) for t in tables],
            pltpu.SemaphoreType.DMA((11,)),
        ],
        compiler_params=pltpu.CompilerParams(
            collective_id=0, has_side_effects=True, vmem_limit_bytes=63 << 20
        ),
        name="sequence_part",
    )(q_proj, k_proj, v_proj, grad_out, long_filter, short_taps, *tables)
    like = jax.ShapeDtypeStruct((rows, width), BF16)
    mixed, gq, gk, gv, gtaps, gh = pl.pallas_call(
        home_kernel,
        out_shape=(
            like, like, like, like,
            jax.ShapeDtypeStruct((3, 3, width), F32),
            jax.ShapeDtypeStruct((rows, width), F32),
        ),
        in_specs=[hbm] * 8,
        out_specs=(hbm,) * 6,
        scratch_shapes=[
            *field,
            *taps,
            *[pltpu.VMEM(value.shape, value.dtype) for value in back],
            pltpu.SemaphoreType.DMA((8,)),
            *field,
            *taps,
            *wide,
            pltpu.SemaphoreType.DMA((4, 6)),
            pltpu.VMEM((2, width, rows), F32),
        ],
        compiler_params=pltpu.CompilerParams(vmem_limit_bytes=63 << 20),
        name="home_part",
    )(q_proj, k_proj, v_proj, grad_out, short_taps, *back)
    return mixed, gq, gk, gv, gtaps, gh


def solution(mesh):
    field = P("ctx", "tp")
    taps = P(None, None, "tp")
    return jax.shard_map(
        local,
        mesh=mesh,
        in_specs=(field, field, field, taps, field, field),
        out_specs=(field, field, field, field, taps, field),
        check_vma=False,
    )
```

```python
import math

import jax
import jax.numpy as jnp
import numpy as np
from jax import lax
from jax.experimental import pallas as pl
from jax.experimental.pallas import tpu as pltpu
from jax.sharding import PartitionSpec as P

F32 = jnp.float32
BF16 = jnp.bfloat16
SLOTS = 16
RANGE = 32768.0
TINY = 1e-30


def encode(value):
    power = value * value
    power = power * power
    power = power * power
    return jnp.where(value < 0.0, -power, power)


def decode(coded):
    size = jnp.abs(coded)
    fourth = lax.rsqrt(lax.rsqrt(size))
    eighth = fourth * lax.rsqrt(fourth)
    return jnp.where(coded < 0.0, -eighth, jnp.where(size > 0.0, eighth, 0.0))


def split_table(table):
    hi = table.astype(BF16)
    return hi, (table - hi.astype(np.float64)).astype(BF16)


def make_tables(parts, rows):
    total = parts * rows
    k1 = np.arange(parts)
    p = np.arange(parts)
    t = np.arange(rows)
    coarse = 2.0 * math.pi * np.outer(k1 + 0.25, p) / parts
    first = np.concatenate([np.cos(coarse), -np.sin(coarse)], axis=0)
    hi, lo = split_table(first)
    first = np.concatenate([hi, hi, lo], axis=1)
    turn = 2.0 * math.pi * np.outer(k1 + 0.25, t) / total
    fine = 2.0 * math.pi * (np.outer(t, t) % rows) / rows
    second = np.block([[np.cos(fine), -np.sin(fine)], [np.sin(fine), np.cos(fine)]])
    hi, lo = split_table(second)
    second = np.concatenate([hi, hi, lo], axis=0)
    last = np.concatenate([np.cos(coarse.T), np.sin(coarse.T)], axis=1) / total
    hi, lo = split_table(last)
    last = np.concatenate([hi, hi, lo], axis=1)
    return first, second, last, np.cos(turn).astype(np.float32), -np.sin(turn).astype(np.float32)


def halves(value):
    hi = value.astype(BF16)
    return hi, (value - hi.astype(F32)).astype(BF16)


def sequence_kernel(
    q_hbm, k_hbm, v_hbm, g_hbm, h_hbm, taps_hbm, first_hbm, second_hbm, last_hbm, cos_hbm, sin_hbm,
    y_in, d_in, notes,
    wave1, wave2, peaks, got1, got2, got_peaks, y_out, d_out, notes_out, taps_t, x, late, feat, fields, spec, conv, lhs,
    send_sem, recv_sem,
    q_ref, k_ref, v_ref, g_ref, h_ref, taps_ref, first_ref, second_ref, last_ref, cos_ref, sin_ref, load_sem,
):
    parts, chans, rows = 64, 8, 128
    width = parts * chans
    me = lax.axis_index("ctx")
    tp = lax.axis_index("tp")
    barrier = pltpu.get_barrier_semaphore()
    loads = [
        pltpu.make_async_copy(source, held, load_sem.at[n])
        for n, (source, held) in enumerate((
            (q_hbm, q_ref), (k_hbm, k_ref), (v_hbm, v_ref), (g_hbm, g_ref), (h_hbm, h_ref), (taps_hbm, taps_ref),
            (first_hbm, first_ref), (second_hbm, second_ref), (last_hbm, last_ref), (cos_hbm, cos_ref), (sin_hbm, sin_ref),
        ))
    ]

    def peer_at(i):
        xi, zi = (i >> 1) & 3, i >> 3
        x_off = 2 + ((xi + 1) >> 1) * (1 - 2 * (xi & 1))
        z_off = 4 + ((zi + 1) >> 1) * (1 - 2 * (zi & 1))
        x_to = ((me >> 4) + x_off) & 3
        y_to = ((me >> 3) & 1) ^ (1 - (i & 1))
        z_to = (me + z_off) & 7
        return (x_to << 4) | (y_to << 3) | z_to

    def span(start, stop, body):
        def step(i, carry):
            body(peer_at(i))
            return carry

        lax.fori_loop(start, stop, step, 0, unroll=9)

    def peers(body):
        span(0, parts - 1, body)

    def target(peer):
        return dict(device_id=(peer, tp), device_id_type=pl.DeviceIdType.MESH)

    peers(lambda peer: pl.semaphore_signal(barrier, inc=1, **target(peer)))
    for load in loads:
        load.start()

    for load in loads[:6]:
        load.wait()

    def turned(ref):
        return jnp.transpose(ref[...].astype(F32)).reshape(parts, chans, rows)

    filt = turned(h_ref)
    peak = jnp.max(jnp.max(jnp.abs(filt), axis=2, keepdims=True), axis=1, keepdims=True)
    peak = jnp.broadcast_to(jnp.maximum(peak, TINY), (parts, 1, rows))
    peaks[...] = peak
    wave1[...] = jnp.concatenate([turned(q_ref), turned(v_ref), encode(filt * (RANGE / peak))], axis=1).astype(BF16)
    wave2[...] = jnp.concatenate([turned(k_ref), turned(g_ref)], axis=1).astype(BF16)
    taps = jnp.concatenate([taps_ref[0], taps_ref[1], taps_ref[2], jnp.zeros((rows - 9, width), F32)], axis=0)
    taps_t[...] = jnp.transpose(taps)

    pl.semaphore_wait(barrier, parts - 1)

    def keep(moves):
        for source, result, n, skip in moves:
            pltpu.make_async_copy(source.at[me + skip], result.at[me], recv_sem.at[n]).start()

    def post(peer, moves):
        for source, result, n, skip in moves:
            pltpu.make_async_remote_copy(
                src_ref=source.at[peer + skip], dst_ref=result.at[me],
                send_sem=send_sem.at[n], recv_sem=recv_sem.at[n], **target(peer)
            ).start()

    def exchange(moves):
        keep(moves)
        peers(lambda peer: post(peer, moves))

    def arrived(result, n):
        pltpu.make_async_copy(result, result, recv_sem.at[n]).wait()

    exchange([(peaks, got_peaks, 1, 0), (wave1, got1, 0, 0)])
    exchange([(wave2, got2, 2, 0)])
    arrived(got1, 0)
    arrived(got_peaks, 1)

    own_taps = taps_t[pl.ds(pl.multiple_of(me * chans, chans), chans), :]

    def tap(s, j):
        return jnp.broadcast_to(own_taps[:, 3 * s + j : 3 * s + j + 1], (chans, rows))[None]

    lane = lax.broadcasted_iota(jnp.int32, (1, chans, rows), 2)
    chunk = 8

    def rolled(value, shift):
        flat = value.reshape(-1, rows)
        return pltpu.roll(flat, shift % rows, axis=1).reshape(value.shape)

    x[:, 0] = jnp.zeros((4, chans, rows), F32)

    def unpack1(i, carry):
        p0 = i * chunk
        here = pl.ds(p0, chunk)
        there = pl.ds(p0 + 1, chunk)
        block = got1[here].astype(F32)
        x[0, there] = block[:, 0:8]
        x[2, there] = block[:, 8:16]
        fields[1, here] = decode(block[:, 16:24]) * (got_peaks[here] * (1.0 / RANGE))
        return carry

    def unpack2(i, carry):
        p0 = i * chunk
        there = pl.ds(p0 + 1, chunk)
        block = got2[pl.ds(p0, chunk)].astype(F32)
        x[1, there] = block[:, 0:8]
        x[3, there] = block[:, 8:16]
        return carry

    lax.fori_loop(0, parts // chunk, unpack1, 0, unroll=True)

    def delayed(s, p0):
        value = x[s, pl.ds(p0, chunk + 1)]
        out = [value[1:]]
        for j in (1, 2):
            moved = rolled(value, j)
            out.append(jnp.where(lane < j, moved[:-1], moved[1:]))
        return out

    def featured(s, p0):
        d = delayed(s, p0)
        here = pl.ds(p0, chunk)
        late[s, 0, here] = d[1]
        late[s, 1, here] = d[2]
        value = tap(s, 0) * d[0] + tap(s, 1) * d[1] + tap(s, 2) * d[2]
        feat[s, here] = value
        return value

    def featurize1(i, carry):
        p0 = i * chunk
        fields[0, pl.ds(p0, chunk)] = featured(0, p0) * featured(2, p0)
        return carry

    def featurize2(i, carry):
        p0 = i * chunk
        fields[2, pl.ds(p0, chunk)] = featured(1, p0) * x[3, pl.ds(p0 + 1, chunk)]
        return carry

    lax.fori_loop(0, parts // chunk, featurize1, 0, unroll=True)

    for load in loads[6:]:
        load.wait()
    turn_re, turn_im = cos_ref[...], sin_ref[...]
    first, second, last = first_ref[...], second_ref[...], last_ref[...]
    flat_fields = fields.reshape(3 * width, rows)
    flat_conv = conv.reshape(3 * width, rows)

    def twiddled(re, im):
        return re * turn_re - im * turn_im, re * turn_im + im * turn_re

    def forward(f):
        for c in range(0, chans, 2):
            pair = [flat_fields[pl.ds(f * width + c + e, parts, stride=chans), :] for e in (0, 1)]
            hi, lo = halves(jnp.concatenate(pair, axis=1))
            mid = jnp.dot(first, jnp.concatenate([hi, lo, hi], axis=0), preferred_element_type=F32)
            for e in (0, 1):
                re, im = twiddled(mid[:parts, e * rows : (e + 1) * rows], mid[parts:, e * rows : (e + 1) * rows])
                hi, lo = halves(jnp.concatenate([re, im], axis=1))
                lhs[f, (c + e) * parts : (c + e + 1) * parts, :] = jnp.concatenate([hi, lo, hi], axis=1)
        spec[f] = jnp.dot(lhs[f], second, preferred_element_type=F32)

    forward(0)
    forward(1)

    def inverse(o):
        f_a, f_b, sign = ((0, 1, 1.0), (2, 1, -1.0), (2, 0, -1.0))[o]
        for c in range(chans):
            block = pl.ds(c * parts, parts)
            a, b = spec[f_a, block, :], spec[f_b, block, :]
            a_re, a_im, b_re, b_im = a[:, :rows], a[:, rows:], b[:, :rows], sign * b[:, rows:]
            re, im = a_re * b_re - a_im * b_im, a_re * b_im + a_im * b_re
            hi, lo = halves(jnp.concatenate([re, -im], axis=1))
            lhs[o, c * parts : (c + 1) * parts, :] = jnp.concatenate([hi, lo, hi], axis=1)
        mid = jnp.dot(lhs[o], second, preferred_element_type=F32)
        for c in range(0, chans, 2):
            pair = []
            for e in (0, 1):
                block = mid[(c + e) * parts : (c + e + 1) * parts]
                pair.append(jnp.concatenate(twiddled(block[:, :rows], block[:, rows:]), axis=0))
            hi, lo = halves(jnp.concatenate(pair, axis=1))
            out = jnp.dot(last, jnp.concatenate([hi, lo, hi], axis=0), preferred_element_type=F32)
            for e in (0, 1):
                flat_conv[pl.ds(o * width + c + e, parts, stride=chans), :] = out[:, e * rows : (e + 1) * rows]

    def scaled(o):
        top = jnp.max(jnp.max(jnp.abs(conv[o]), axis=0), axis=1, keepdims=True)
        top = jnp.broadcast_to(jnp.maximum(top, TINY), (chans, rows))
        return top, (RANGE / top)[None]

    inverse(0)
    y_peak, y_gain = scaled(0)

    def code_y(i, carry):
        here = pl.ds(i * chunk, chunk)
        y_out[here] = encode(conv[0, here] * y_gain).astype(BF16)
        return carry

    lax.fori_loop(0, parts // chunk, code_y, 0, unroll=True)
    exchange([(y_out, y_in, 3, 0)])

    arrived(got2, 2)
    lax.fori_loop(0, parts // chunk, unpack2, 0, unroll=True)
    lax.fori_loop(0, parts // chunk, featurize2, 0, unroll=True)
    forward(2)
    inverse(1)
    inverse(2)
    dz_peak, dz_gain = scaled(1)
    dh_peak, dh_gain = scaled(2)
    peak = (y_peak, dz_peak, dh_peak)

    def code_d(i, carry):
        here = pl.ds(i * chunk, chunk)
        pair = [encode(conv[1, here] * dz_gain), encode(conv[2, here] * dh_gain)]
        d_out[here] = jnp.concatenate(pair, axis=1).astype(BF16)
        return carry

    lax.fori_loop(0, parts // chunk, code_d, 0, unroll=True)
    group = lax.broadcasted_iota(jnp.int32, (1, chans, rows), 2) // SLOTS
    sublane = lax.broadcasted_iota(jnp.int32, (1, chans, rows), 1)

    def flattened(value):
        for shift in (SLOTS, 2 * SLOTS, 4 * SLOTS):
            value = value + rolled(value, shift)
        return jnp.sum(jnp.where(group == sublane, value, 0.0), axis=1, keepdims=True)

    def placed(values, lane0):
        out = jnp.zeros_like(values[0])
        for n, value in enumerate(values):
            at = lane0 + 2 * n
            out = jnp.where((lane >= at) & (lane < at + 2), rolled(value, at) if at else value, out)
        return out

    def tally(i, sums):
        p0 = i * chunk
        here = pl.ds(p0, chunk)
        there = pl.ds(p0 + 1, chunk)
        y, dz = conv[0, here], conv[1, here]
        a = [feat[s, here] for s in range(3)]
        da = [dz * a[2], x[3, there] * y, dz * a[0]]
        sums = list(sums)
        for s in range(3):
            d = (x[s, there], late[s, 0, here], late[s, 1, here])
            for j in range(3):
                sums[3 * s + j] = sums[3 * s + j] + jnp.sum(da[s] * d[j], axis=0)
        notes_out[here, 0:1, :] = flattened(placed(da, 9))
        notes_out[there, 1:2, :] = flattened(placed(a, 0))
        return tuple(sums)

    sums = (jnp.zeros((chans, rows), F32),) * 9
    d_moves = [(d_out, d_in, 4, 0)]
    for i in range(parts // chunk):
        sums = tally(i, sums)
    notes_out[parts, 0:1, :] = jnp.zeros((1, rows), F32)
    lane2 = lane[0]
    first_note = jnp.zeros((chans, rows), F32)
    for n in range(9):
        first_note = jnp.where(lane2 == n, jnp.sum(sums[n], axis=1, keepdims=True), first_note)
    second_note = jnp.zeros((chans, rows), F32)
    for o in range(3):
        second_note = jnp.where(lane2 == 6 + o, peak[o], second_note)
    both = jnp.concatenate([flattened(first_note[None]), flattened(second_note[None])], axis=1)
    later = pl.ds(1, parts)
    notes_out[later] = notes_out[later] + both

    note_moves = [(notes_out, notes, 5, 1)]
    peers(lambda peer: post(peer, note_moves + d_moves))
    keep(d_moves + note_moves)
    arrived(y_in, 3)
    arrived(d_in, 4)
    arrived(notes, 5)
    for n, source in enumerate((wave1, peaks, wave2, y_out, d_out, notes_out)):
        sent = source.at[pl.ds(0, parts - 1)]
        pltpu.make_async_copy(sent, sent, send_sem.at[n]).wait()


def home_kernel(
    q_hbm, k_hbm, v_hbm, g_hbm, taps_hbm, y_hbm, d_hbm, notes_hbm,
    mixed_hbm, gq_hbm, gk_hbm, gv_hbm, gtaps_hbm, gh_hbm,
    q_ref, k_ref, v_ref, g_ref, taps_ref, y_ref, d_ref, notes_ref, load_sem,
    mixed_ref, gq_ref, gk_ref, gv_ref, gtaps_ref, gh_ref, store_sem,
    notes_t,
):
    parts, chans, rows = 64, 8, 128
    loads = [
        pltpu.make_async_copy(source, held, load_sem.at[n])
        for n, (source, held) in enumerate((
            (notes_hbm, notes_ref), (y_hbm, y_ref), (d_hbm, d_ref), (taps_hbm, taps_ref),
            (q_hbm, q_ref), (k_hbm, k_ref), (v_hbm, v_ref), (g_hbm, g_ref),
        ))
    ]
    for load in loads:
        load.start()
    results = (
        (gtaps_ref, gtaps_hbm), (gh_ref, gh_hbm), (mixed_ref, mixed_hbm), (gq_ref, gq_hbm), (gk_ref, gk_hbm), (gv_ref, gv_hbm),
    )
    stores = []
    loads[0].wait()
    for r in range(2):
        note = notes_ref[:, r, :]
        for c in range(chans):
            notes_t[r, pl.ds(c, parts, stride=chans), :] = pltpu.roll(note, (rows - SLOTS * c) % rows, axis=1) if c else note
    for load in loads[1:]:
        load.wait()
    row = lax.broadcasted_iota(jnp.int32, (rows, rows), 0)
    inputs = (q_ref, k_ref, v_ref)
    outputs = (gq_ref, gk_ref, gv_ref)
    pad = jnp.zeros((8, rows), F32)
    for b in range(4):
        cols = slice(b * rows, (b + 1) * rows)
        groups = slice(b * 16, (b + 1) * 16)
        note = [jnp.transpose(notes_t[r, cols, :])[0:16] for r in range(2)]
        for s in range(3):
            gtaps_ref[s, :, cols] = note[0][3 * s : 3 * s + 3]
        pair = decode(d_ref[groups].astype(F32))
        y, dz, dh = [
            jnp.transpose(value.reshape(rows, rows)) * (note[1][6 + o : 7 + o] * (1.0 / RANGE))
            for o, value in enumerate((decode(y_ref[groups].astype(F32)), pair[:, 0:8], pair[:, 8:16]))
        ]
        gh_ref[:, cols] = dh
        tap = [[taps_ref[s, j : j + 1, cols] for j in range(3)] for s in range(3)]
        a = []
        for s in range(3):
            value = inputs[s][:, cols].astype(F32)
            joined = jnp.concatenate([pad, value], axis=0)
            total = tap[s][0] * value + tap[s][1] * joined[7 : 7 + rows] + tap[s][2] * joined[6 : 6 + rows]
            total = jnp.where(row == 0, note[1][2 * s : 2 * s + 1], total)
            a.append(jnp.where(row == 1, note[1][2 * s + 1 : 2 * s + 2], total))
        mixed_ref[:, cols] = (a[1] * y).astype(BF16)
        da = [dz * a[2], g_ref[:, cols].astype(F32) * y, dz * a[0]]
        for s in range(3):
            joined = jnp.concatenate([da[s], note[0][9 + 2 * s : 11 + 2 * s], pad[0:6]], axis=0)
            total = tap[s][0] * da[s] + tap[s][1] * joined[1 : 1 + rows] + tap[s][2] * joined[2 : 2 + rows]
            outputs[s][:, cols] = total.astype(BF16)
        for n, (held, result) in enumerate(results):
            block = (slice(None),) * (len(held.shape) - 1) + (cols,)
            store = pltpu.make_async_copy(held.at[block], result.at[block], store_sem.at[b, n])
            store.start()
            stores.append(store)
    for store in stores:
        store.wait()


def local(q_proj, k_proj, v_proj, short_taps, long_filter, grad_out):
    parts = lax.axis_size("ctx")
    rows, width = q_proj.shape
    chans = width // parts
    tables = [jnp.asarray(t) for t in make_tables(parts, rows)]
    hbm = pl.BlockSpec(memory_space=pltpu.HBM)
    field = [pltpu.VMEM((rows, width), BF16) for _ in range(4)]
    wide = [pltpu.VMEM((rows, width), F32)]
    taps = [pltpu.VMEM((3, 3, width), F32)]
    y_all = jax.ShapeDtypeStruct((parts, chans, rows), BF16)
    d_all = jax.ShapeDtypeStruct((parts, 2 * chans, rows), BF16)
    notes = jax.ShapeDtypeStruct((parts, 2, rows), F32)
    back = pl.pallas_call(
        sequence_kernel,
        out_shape=(y_all, d_all, notes),
        in_specs=[hbm] * 11,
        out_specs=(hbm,) * 3,
        scratch_shapes=[
            *[
                pltpu.VMEM((parts, 3 * chans, rows), BF16),
                pltpu.VMEM((parts, 2 * chans, rows), BF16),
                pltpu.VMEM((parts, 1, rows), F32),
            ] * 2,
            pltpu.VMEM(y_all.shape, BF16),
            pltpu.VMEM(d_all.shape, BF16),
            pltpu.VMEM((parts + 1, 2, rows), F32),
            pltpu.VMEM((width, rows), F32),
            pltpu.VMEM((4, parts + 1, chans, rows), F32),
            pltpu.VMEM((3, 2, parts, chans, rows), F32),
            pltpu.VMEM((3, parts, chans, rows), F32),
            pltpu.VMEM((3, parts, chans, rows), F32),
            pltpu.VMEM((3, width, 2 * rows), F32),
            pltpu.VMEM((3, parts, chans, rows), F32),
            pltpu.VMEM((3, width, 6 * rows), BF16),
            *[pltpu.SemaphoreType.DMA((6,))] * 2,
            *field,
            *wide,
            *taps,
            *[pltpu.VMEM(t.shape, t.dtype) for t in tables],
            pltpu.SemaphoreType.DMA((11,)),
        ],
        compiler_params=pltpu.CompilerParams(
            collective_id=0, has_side_effects=True, vmem_limit_bytes=63 << 20
        ),
        name="sequence_part",
    )(q_proj, k_proj, v_proj, grad_out, long_filter, short_taps, *tables)
    like = jax.ShapeDtypeStruct((rows, width), BF16)
    mixed, gq, gk, gv, gtaps, gh = pl.pallas_call(
        home_kernel,
        out_shape=(
            like, like, like, like,
            jax.ShapeDtypeStruct((3, 3, width), F32),
            jax.ShapeDtypeStruct((rows, width), F32),
        ),
        in_specs=[hbm] * 8,
        out_specs=(hbm,) * 6,
        scratch_shapes=[
            *field,
            *taps,
            *[pltpu.VMEM(value.shape, value.dtype) for value in back],
            pltpu.SemaphoreType.DMA((8,)),
            *field,
            *taps,
            *wide,
            pltpu.SemaphoreType.DMA((4, 6)),
            pltpu.VMEM((2, width, rows), F32),
        ],
        compiler_params=pltpu.CompilerParams(vmem_limit_bytes=63 << 20),
        name="home_part",
    )(q_proj, k_proj, v_proj, grad_out, short_taps, *back)
    return mixed, gq, gk, gv, gtaps, gh


def solution(mesh):
    field = P("ctx", "tp")
    taps = P(None, None, "tp")
    return jax.shard_map(
        local,
        mesh=mesh,
        in_specs=(field, field, field, taps, field, field),
        out_specs=(field, field, field, field, taps, field),
        check_vma=False,
    )
```

```python
import math

import jax
import jax.numpy as jnp
import numpy as np
from jax import lax
from jax.experimental import pallas as pl
from jax.experimental.pallas import tpu as pltpu
from jax.sharding import PartitionSpec as P

F32 = jnp.float32
BF16 = jnp.bfloat16
SLOTS = 16
RANGE = 32768.0
TINY = 1e-30


def encode(value):
    power = value * value
    power = power * power
    power = power * power
    return jnp.where(value < 0.0, -power, power)


def decode(coded):
    size = jnp.abs(coded)
    fourth = lax.rsqrt(lax.rsqrt(size))
    eighth = fourth * lax.rsqrt(fourth)
    return jnp.where(coded < 0.0, -eighth, jnp.where(size > 0.0, eighth, 0.0))


def split_table(table):
    hi = table.astype(BF16)
    return hi, (table - hi.astype(np.float64)).astype(BF16)


def make_tables(parts, rows):
    total = parts * rows
    k1 = np.arange(parts)
    p = np.arange(parts)
    t = np.arange(rows)
    coarse = 2.0 * math.pi * np.outer(k1 + 0.25, p) / parts
    first = np.concatenate([np.cos(coarse), -np.sin(coarse)], axis=0)
    hi, lo = split_table(first)
    first = np.concatenate([hi, hi, lo], axis=1)
    turn = 2.0 * math.pi * np.outer(k1 + 0.25, t) / total
    fine = 2.0 * math.pi * (np.outer(t, t) % rows) / rows
    second = np.block([[np.cos(fine), -np.sin(fine)], [np.sin(fine), np.cos(fine)]])
    hi, lo = split_table(second)
    second = np.concatenate([hi, hi, lo], axis=0)
    last = np.concatenate([np.cos(coarse.T), np.sin(coarse.T)], axis=1) / total
    hi, lo = split_table(last)
    last = np.concatenate([hi, hi, lo], axis=1)
    return first, second, last, np.cos(turn).astype(np.float32), -np.sin(turn).astype(np.float32)


def halves(value):
    hi = value.astype(BF16)
    return hi, (value - hi.astype(F32)).astype(BF16)


def sequence_kernel(
    q_hbm, k_hbm, v_hbm, g_hbm, h_hbm, taps_hbm, first_hbm, second_hbm, last_hbm, cos_hbm, sin_hbm,
    y_in, d_in, notes,
    wave1, wave2, peaks, got1, got2, got_peaks, y_out, d_out, notes_out, taps_t, x, late, feat, fields, spec, conv, lhs,
    send_sem, recv_sem,
    q_ref, k_ref, v_ref, g_ref, h_ref, taps_ref, first_ref, second_ref, last_ref, cos_ref, sin_ref, load_sem,
):
    parts, chans, rows = 64, 8, 128
    width = parts * chans
    me = lax.axis_index("ctx")
    tp = lax.axis_index("tp")
    barrier = pltpu.get_barrier_semaphore()
    loads = [
        pltpu.make_async_copy(source, held, load_sem.at[n])
        for n, (source, held) in enumerate((
            (q_hbm, q_ref), (k_hbm, k_ref), (v_hbm, v_ref), (g_hbm, g_ref), (h_hbm, h_ref), (taps_hbm, taps_ref),
            (first_hbm, first_ref), (second_hbm, second_ref), (last_hbm, last_ref), (cos_hbm, cos_ref), (sin_hbm, sin_ref),
        ))
    ]

    def peer_at(i):
        xi, zi = (i >> 1) & 3, i >> 3
        x_off = 2 + ((xi + 1) >> 1) * (1 - 2 * (xi & 1))
        z_off = 4 + ((zi + 1) >> 1) * (1 - 2 * (zi & 1))
        x_to = ((me >> 4) + x_off) & 3
        y_to = ((me >> 3) & 1) ^ (1 - (i & 1))
        z_to = (me + z_off) & 7
        return (x_to << 4) | (y_to << 3) | z_to

    def span(start, stop, body):
        def step(i, carry):
            body(peer_at(i))
            return carry

        lax.fori_loop(start, stop, step, 0, unroll=9)

    def peers(body):
        span(0, parts - 1, body)

    def target(peer):
        return dict(device_id=(peer, tp), device_id_type=pl.DeviceIdType.MESH)

    for load in loads[:6]:
        load.start()
    peers(lambda peer: pl.semaphore_signal(barrier, inc=1, **target(peer)))
    for load in loads[6:]:
        load.start()

    for load in loads[:6]:
        load.wait()

    def turned(ref):
        return jnp.transpose(ref[...].astype(F32)).reshape(parts, chans, rows)

    filt = turned(h_ref)
    peak = jnp.max(jnp.max(jnp.abs(filt), axis=2, keepdims=True), axis=1, keepdims=True)
    peak = jnp.broadcast_to(jnp.maximum(peak, TINY), (parts, 1, rows))
    peaks[...] = peak
    wave1[...] = jnp.concatenate([turned(q_ref), turned(v_ref), encode(filt * (RANGE / peak))], axis=1).astype(BF16)
    wave2[...] = jnp.concatenate([turned(k_ref), turned(g_ref)], axis=1).astype(BF16)
    taps = jnp.concatenate([taps_ref[0], taps_ref[1], taps_ref[2], jnp.zeros((rows - 9, width), F32)], axis=0)
    taps_t[...] = jnp.transpose(taps)

    pl.semaphore_wait(barrier, parts - 1)

    def keep(moves):
        for source, result, n, skip in moves:
            pltpu.make_async_copy(source.at[me + skip], result.at[me], recv_sem.at[n]).start()

    def post(peer, moves):
        for source, result, n, skip in moves:
            pltpu.make_async_remote_copy(
                src_ref=source.at[peer + skip], dst_ref=result.at[me],
                send_sem=send_sem.at[n], recv_sem=recv_sem.at[n], **target(peer)
            ).start()

    def exchange(moves):
        keep(moves)
        peers(lambda peer: post(peer, moves))

    def arrived(result, n):
        pltpu.make_async_copy(result, result, recv_sem.at[n]).wait()

    exchange([(peaks, got_peaks, 1, 0), (wave1, got1, 0, 0)])
    exchange([(wave2, got2, 2, 0)])
    arrived(got1, 0)
    arrived(got_peaks, 1)

    own_taps = taps_t[pl.ds(pl.multiple_of(me * chans, chans), chans), :]

    def tap(s, j):
        return jnp.broadcast_to(own_taps[:, 3 * s + j : 3 * s + j + 1], (chans, rows))[None]

    lane = lax.broadcasted_iota(jnp.int32, (1, chans, rows), 2)
    chunk = 8

    def rolled(value, shift):
        flat = value.reshape(-1, rows)
        return pltpu.roll(flat, shift % rows, axis=1).reshape(value.shape)

    x[:, 0] = jnp.zeros((4, chans, rows), F32)

    def unpack1(i, carry):
        p0 = i * chunk
        here = pl.ds(p0, chunk)
        there = pl.ds(p0 + 1, chunk)
        block = got1[here].astype(F32)
        x[0, there] = block[:, 0:8]
        x[2, there] = block[:, 8:16]
        fields[1, here] = decode(block[:, 16:24]) * (got_peaks[here] * (1.0 / RANGE))
        return carry

    def unpack2(i, carry):
        p0 = i * chunk
        there = pl.ds(p0 + 1, chunk)
        block = got2[pl.ds(p0, chunk)].astype(F32)
        x[1, there] = block[:, 0:8]
        x[3, there] = block[:, 8:16]
        return carry

    lax.fori_loop(0, parts // chunk, unpack1, 0, unroll=True)

    def delayed(s, p0):
        value = x[s, pl.ds(p0, chunk + 1)]
        out = [value[1:]]
        for j in (1, 2):
            moved = rolled(value, j)
            out.append(jnp.where(lane < j, moved[:-1], moved[1:]))
        return out

    def featured(s, p0):
        d = delayed(s, p0)
        here = pl.ds(p0, chunk)
        late[s, 0, here] = d[1]
        late[s, 1, here] = d[2]
        value = tap(s, 0) * d[0] + tap(s, 1) * d[1] + tap(s, 2) * d[2]
        feat[s, here] = value
        return value

    def featurize1(i, carry):
        p0 = i * chunk
        fields[0, pl.ds(p0, chunk)] = featured(0, p0) * featured(2, p0)
        return carry

    def featurize2(i, carry):
        p0 = i * chunk
        fields[2, pl.ds(p0, chunk)] = featured(1, p0) * x[3, pl.ds(p0 + 1, chunk)]
        return carry

    lax.fori_loop(0, parts // chunk, featurize1, 0, unroll=True)

    for load in loads[6:]:
        load.wait()
    turn_re, turn_im = cos_ref[...], sin_ref[...]
    first, second, last = first_ref[...], second_ref[...], last_ref[...]
    flat_fields = fields.reshape(3 * width, rows)
    flat_conv = conv.reshape(3 * width, rows)

    def twiddled(re, im):
        return re * turn_re - im * turn_im, re * turn_im + im * turn_re

    def forward(f):
        for c in range(0, chans, 2):
            pair = [flat_fields[pl.ds(f * width + c + e, parts, stride=chans), :] for e in (0, 1)]
            hi, lo = halves(jnp.concatenate(pair, axis=1))
            mid = jnp.dot(first, jnp.concatenate([hi, lo, hi], axis=0), preferred_element_type=F32)
            for e in (0, 1):
                re, im = twiddled(mid[:parts, e * rows : (e + 1) * rows], mid[parts:, e * rows : (e + 1) * rows])
                hi, lo = halves(jnp.concatenate([re, im], axis=1))
                lhs[f, (c + e) * parts : (c + e + 1) * parts, :] = jnp.concatenate([hi, lo, hi], axis=1)
        spec[f] = jnp.dot(lhs[f], second, preferred_element_type=F32)

    forward(0)
    forward(1)

    def inverse(o):
        f_a, f_b, sign = ((0, 1, 1.0), (2, 1, -1.0), (2, 0, -1.0))[o]
        for c in range(chans):
            block = pl.ds(c * parts, parts)
            a, b = spec[f_a, block, :], spec[f_b, block, :]
            a_re, a_im, b_re, b_im = a[:, :rows], a[:, rows:], b[:, :rows], sign * b[:, rows:]
            re, im = a_re * b_re - a_im * b_im, a_re * b_im + a_im * b_re
            hi, lo = halves(jnp.concatenate([re, -im], axis=1))
            lhs[o, c * parts : (c + 1) * parts, :] = jnp.concatenate([hi, lo, hi], axis=1)
        mid = jnp.dot(lhs[o], second, preferred_element_type=F32)
        for c in range(0, chans, 2):
            pair = []
            for e in (0, 1):
                block = mid[(c + e) * parts : (c + e + 1) * parts]
                pair.append(jnp.concatenate(twiddled(block[:, :rows], block[:, rows:]), axis=0))
            hi, lo = halves(jnp.concatenate(pair, axis=1))
            out = jnp.dot(last, jnp.concatenate([hi, lo, hi], axis=0), preferred_element_type=F32)
            for e in (0, 1):
                flat_conv[pl.ds(o * width + c + e, parts, stride=chans), :] = out[:, e * rows : (e + 1) * rows]

    def scaled(o):
        top = jnp.max(jnp.max(jnp.abs(conv[o]), axis=0), axis=1, keepdims=True)
        top = jnp.broadcast_to(jnp.maximum(top, TINY), (chans, rows))
        return top, (RANGE / top)[None]

    inverse(0)
    y_peak, y_gain = scaled(0)

    def code_y(i, carry):
        here = pl.ds(i * chunk, chunk)
        y_out[here] = encode(conv[0, here] * y_gain).astype(BF16)
        return carry

    lax.fori_loop(0, parts // chunk, code_y, 0, unroll=True)
    exchange([(y_out, y_in, 3, 0)])

    arrived(got2, 2)
    lax.fori_loop(0, parts // chunk, unpack2, 0, unroll=True)
    lax.fori_loop(0, parts // chunk, featurize2, 0, unroll=True)
    forward(2)
    inverse(1)
    inverse(2)
    dz_peak, dz_gain = scaled(1)
    dh_peak, dh_gain = scaled(2)
    peak = (y_peak, dz_peak, dh_peak)

    def code_d(i, carry):
        here = pl.ds(i * chunk, chunk)
        pair = [encode(conv[1, here] * dz_gain), encode(conv[2, here] * dh_gain)]
        d_out[here] = jnp.concatenate(pair, axis=1).astype(BF16)
        return carry

    lax.fori_loop(0, parts // chunk, code_d, 0, unroll=True)
    group = lax.broadcasted_iota(jnp.int32, (1, chans, rows), 2) // SLOTS
    sublane = lax.broadcasted_iota(jnp.int32, (1, chans, rows), 1)

    def flattened(value):
        for shift in (SLOTS, 2 * SLOTS, 4 * SLOTS):
            value = value + rolled(value, shift)
        return jnp.sum(jnp.where(group == sublane, value, 0.0), axis=1, keepdims=True)

    def placed(values, lane0):
        out = jnp.zeros_like(values[0])
        for n, value in enumerate(values):
            at = lane0 + 2 * n
            out = jnp.where((lane >= at) & (lane < at + 2), rolled(value, at) if at else value, out)
        return out

    def tally(i, sums):
        p0 = i * chunk
        here = pl.ds(p0, chunk)
        there = pl.ds(p0 + 1, chunk)
        y, dz = conv[0, here], conv[1, here]
        a = [feat[s, here] for s in range(3)]
        da = [dz * a[2], x[3, there] * y, dz * a[0]]
        sums = list(sums)
        for s in range(3):
            d = (x[s, there], late[s, 0, here], late[s, 1, here])
            for j in range(3):
                sums[3 * s + j] = sums[3 * s + j] + jnp.sum(da[s] * d[j], axis=0)
        notes_out[here, 0:1, :] = flattened(placed(da, 9))
        notes_out[there, 1:2, :] = flattened(placed(a, 0))
        return tuple(sums)

    sums = (jnp.zeros((chans, rows), F32),) * 9
    d_moves = [(d_out, d_in, 4, 0)]
    for i in range(parts // chunk):
        sums = tally(i, sums)
    notes_out[parts, 0:1, :] = jnp.zeros((1, rows), F32)
    lane2 = lane[0]
    first_note = jnp.zeros((chans, rows), F32)
    for n in range(9):
        first_note = jnp.where(lane2 == n, jnp.sum(sums[n], axis=1, keepdims=True), first_note)
    second_note = jnp.zeros((chans, rows), F32)
    for o in range(3):
        second_note = jnp.where(lane2 == 6 + o, peak[o], second_note)
    both = jnp.concatenate([flattened(first_note[None]), flattened(second_note[None])], axis=1)
    later = pl.ds(1, parts)
    notes_out[later] = notes_out[later] + both

    note_moves = [(notes_out, notes, 5, 1)]
    peers(lambda peer: post(peer, note_moves + d_moves))
    keep(d_moves + note_moves)
    arrived(y_in, 3)
    arrived(d_in, 4)
    arrived(notes, 5)
    for n, source in enumerate((wave1, peaks, wave2, y_out, d_out, notes_out)):
        sent = source.at[pl.ds(0, parts - 1)]
        pltpu.make_async_copy(sent, sent, send_sem.at[n]).wait()


def home_kernel(
    q_hbm, k_hbm, v_hbm, g_hbm, taps_hbm, y_hbm, d_hbm, notes_hbm,
    mixed_hbm, gq_hbm, gk_hbm, gv_hbm, gtaps_hbm, gh_hbm,
    q_ref, k_ref, v_ref, g_ref, taps_ref, y_ref, d_ref, notes_ref, load_sem,
    mixed_ref, gq_ref, gk_ref, gv_ref, gtaps_ref, gh_ref, store_sem,
    notes_t,
):
    parts, chans, rows = 64, 8, 128
    loads = [
        pltpu.make_async_copy(source, held, load_sem.at[n])
        for n, (source, held) in enumerate((
            (notes_hbm, notes_ref), (y_hbm, y_ref), (d_hbm, d_ref), (taps_hbm, taps_ref),
            (q_hbm, q_ref), (k_hbm, k_ref), (v_hbm, v_ref), (g_hbm, g_ref),
        ))
    ]
    for load in loads:
        load.start()
    results = (
        (gtaps_ref, gtaps_hbm), (gh_ref, gh_hbm), (mixed_ref, mixed_hbm), (gq_ref, gq_hbm), (gk_ref, gk_hbm), (gv_ref, gv_hbm),
    )
    stores = []
    loads[0].wait()
    for r in range(2):
        note = notes_ref[:, r, :]
        for c in range(chans):
            notes_t[r, pl.ds(c, parts, stride=chans), :] = pltpu.roll(note, (rows - SLOTS * c) % rows, axis=1) if c else note
    for load in loads[1:]:
        load.wait()
    row = lax.broadcasted_iota(jnp.int32, (rows, rows), 0)
    inputs = (q_ref, k_ref, v_ref)
    outputs = (gq_ref, gk_ref, gv_ref)
    pad = jnp.zeros((8, rows), F32)
    for b in range(4):
        cols = slice(b * rows, (b + 1) * rows)
        groups = slice(b * 16, (b + 1) * 16)
        note = [jnp.transpose(notes_t[r, cols, :])[0:16] for r in range(2)]
        for s in range(3):
            gtaps_ref[s, :, cols] = note[0][3 * s : 3 * s + 3]
        pair = decode(d_ref[groups].astype(F32))
        y, dz, dh = [
            jnp.transpose(value.reshape(rows, rows)) * (note[1][6 + o : 7 + o] * (1.0 / RANGE))
            for o, value in enumerate((decode(y_ref[groups].astype(F32)), pair[:, 0:8], pair[:, 8:16]))
        ]
        gh_ref[:, cols] = dh
        tap = [[taps_ref[s, j : j + 1, cols] for j in range(3)] for s in range(3)]
        a = []
        for s in range(3):
            value = inputs[s][:, cols].astype(F32)
            joined = jnp.concatenate([pad, value], axis=0)
            total = tap[s][0] * value + tap[s][1] * joined[7 : 7 + rows] + tap[s][2] * joined[6 : 6 + rows]
            total = jnp.where(row == 0, note[1][2 * s : 2 * s + 1], total)
            a.append(jnp.where(row == 1, note[1][2 * s + 1 : 2 * s + 2], total))
        mixed_ref[:, cols] = (a[1] * y).astype(BF16)
        da = [dz * a[2], g_ref[:, cols].astype(F32) * y, dz * a[0]]
        for s in range(3):
            joined = jnp.concatenate([da[s], note[0][9 + 2 * s : 11 + 2 * s], pad[0:6]], axis=0)
            total = tap[s][0] * da[s] + tap[s][1] * joined[1 : 1 + rows] + tap[s][2] * joined[2 : 2 + rows]
            outputs[s][:, cols] = total.astype(BF16)
        for n, (held, result) in enumerate(results):
            block = (slice(None),) * (len(held.shape) - 1) + (cols,)
            store = pltpu.make_async_copy(held.at[block], result.at[block], store_sem.at[b, n])
            store.start()
            stores.append(store)
    for store in stores:
        store.wait()


def local(q_proj, k_proj, v_proj, short_taps, long_filter, grad_out):
    parts = lax.axis_size("ctx")
    rows, width = q_proj.shape
    chans = width // parts
    tables = [jnp.asarray(t) for t in make_tables(parts, rows)]
    hbm = pl.BlockSpec(memory_space=pltpu.HBM)
    field = [pltpu.VMEM((rows, width), BF16) for _ in range(4)]
    wide = [pltpu.VMEM((rows, width), F32)]
    taps = [pltpu.VMEM((3, 3, width), F32)]
    y_all = jax.ShapeDtypeStruct((parts, chans, rows), BF16)
    d_all = jax.ShapeDtypeStruct((parts, 2 * chans, rows), BF16)
    notes = jax.ShapeDtypeStruct((parts, 2, rows), F32)
    back = pl.pallas_call(
        sequence_kernel,
        out_shape=(y_all, d_all, notes),
        in_specs=[hbm] * 11,
        out_specs=(hbm,) * 3,
        scratch_shapes=[
            *[
                pltpu.VMEM((parts, 3 * chans, rows), BF16),
                pltpu.VMEM((parts, 2 * chans, rows), BF16),
                pltpu.VMEM((parts, 1, rows), F32),
            ] * 2,
            pltpu.VMEM(y_all.shape, BF16),
            pltpu.VMEM(d_all.shape, BF16),
            pltpu.VMEM((parts + 1, 2, rows), F32),
            pltpu.VMEM((width, rows), F32),
            pltpu.VMEM((4, parts + 1, chans, rows), F32),
            pltpu.VMEM((3, 2, parts, chans, rows), F32),
            pltpu.VMEM((3, parts, chans, rows), F32),
            pltpu.VMEM((3, parts, chans, rows), F32),
            pltpu.VMEM((3, width, 2 * rows), F32),
            pltpu.VMEM((3, parts, chans, rows), F32),
            pltpu.VMEM((3, width, 6 * rows), BF16),
            *[pltpu.SemaphoreType.DMA((6,))] * 2,
            *field,
            *wide,
            *taps,
            *[pltpu.VMEM(t.shape, t.dtype) for t in tables],
            pltpu.SemaphoreType.DMA((11,)),
        ],
        compiler_params=pltpu.CompilerParams(
            collective_id=0, has_side_effects=True, vmem_limit_bytes=63 << 20
        ),
        name="sequence_part",
    )(q_proj, k_proj, v_proj, grad_out, long_filter, short_taps, *tables)
    like = jax.ShapeDtypeStruct((rows, width), BF16)
    mixed, gq, gk, gv, gtaps, gh = pl.pallas_call(
        home_kernel,
        out_shape=(
            like, like, like, like,
            jax.ShapeDtypeStruct((3, 3, width), F32),
            jax.ShapeDtypeStruct((rows, width), F32),
        ),
        in_specs=[hbm] * 8,
        out_specs=(hbm,) * 6,
        scratch_shapes=[
            *field,
            *taps,
            *[pltpu.VMEM(value.shape, value.dtype) for value in back],
            pltpu.SemaphoreType.DMA((8,)),
            *field,
            *taps,
            *wide,
            pltpu.SemaphoreType.DMA((4, 6)),
            pltpu.VMEM((2, width, rows), F32),
        ],
        compiler_params=pltpu.CompilerParams(vmem_limit_bytes=63 << 20),
        name="home_part",
    )(q_proj, k_proj, v_proj, grad_out, short_taps, *back)
    return mixed, gq, gk, gv, gtaps, gh


def solution(mesh):
    field = P("ctx", "tp")
    taps = P(None, None, "tp")
    return jax.shard_map(
        local,
        mesh=mesh,
        in_specs=(field, field, field, taps, field, field),
        out_specs=(field, field, field, field, taps, field),
        check_vma=False,
    )
```

```python
import math

import jax
import jax.numpy as jnp
import numpy as np
from jax import lax
from jax.experimental import pallas as pl
from jax.experimental.pallas import tpu as pltpu
from jax.sharding import PartitionSpec as P

F32 = jnp.float32
BF16 = jnp.bfloat16
SLOTS = 16
RANGE = 32768.0
TINY = 1e-30


def encode(value):
    power = value * value
    power = power * power
    power = power * power
    return jnp.where(value < 0.0, -power, power)


def decode(coded):
    size = jnp.abs(coded)
    fourth = lax.rsqrt(lax.rsqrt(size))
    eighth = fourth * lax.rsqrt(fourth)
    return jnp.where(coded < 0.0, -eighth, jnp.where(size > 0.0, eighth, 0.0))


def split_table(table):
    hi = table.astype(BF16)
    return hi, (table - hi.astype(np.float64)).astype(BF16)


def make_tables(parts, rows):
    total = parts * rows
    k1 = np.arange(parts)
    p = np.arange(parts)
    t = np.arange(rows)
    coarse = 2.0 * math.pi * np.outer(k1 + 0.25, p) / parts
    first = np.concatenate([np.cos(coarse), -np.sin(coarse)], axis=0)
    hi, lo = split_table(first)
    first = np.concatenate([hi, hi, lo], axis=1)
    turn = 2.0 * math.pi * np.outer(k1 + 0.25, t) / total
    fine = 2.0 * math.pi * (np.outer(t, t) % rows) / rows
    second = np.block([[np.cos(fine), -np.sin(fine)], [np.sin(fine), np.cos(fine)]])
    hi, lo = split_table(second)
    second = np.concatenate([hi, hi, lo], axis=0)
    last = np.concatenate([np.cos(coarse.T), np.sin(coarse.T)], axis=1) / total
    hi, lo = split_table(last)
    last = np.concatenate([hi, hi, lo], axis=1)
    return first, second, last, np.cos(turn).astype(np.float32), -np.sin(turn).astype(np.float32)


def halves(value):
    hi = value.astype(BF16)
    return hi, (value - hi.astype(F32)).astype(BF16)


def sequence_kernel(
    q_hbm, k_hbm, v_hbm, g_hbm, h_hbm, taps_hbm, first_hbm, second_hbm, last_hbm, cos_hbm, sin_hbm,
    y_in, d_in, notes,
    wave1, wave2, peaks, got1, got2, got_peaks, y_out, d_out, notes_out, taps_t, x, late, feat, fields, spec, conv, lhs,
    send_sem, recv_sem,
    q_ref, k_ref, v_ref, g_ref, h_ref, taps_ref, first_ref, second_ref, last_ref, cos_ref, sin_ref, load_sem,
):
    parts, chans, rows = 64, 8, 128
    width = parts * chans
    me = lax.axis_index("ctx")
    tp = lax.axis_index("tp")
    barrier = pltpu.get_barrier_semaphore()
    loads = [
        pltpu.make_async_copy(source, held, load_sem.at[n])
        for n, (source, held) in enumerate((
            (q_hbm, q_ref), (k_hbm, k_ref), (v_hbm, v_ref), (g_hbm, g_ref), (h_hbm, h_ref), (taps_hbm, taps_ref),
            (first_hbm, first_ref), (second_hbm, second_ref), (last_hbm, last_ref), (cos_hbm, cos_ref), (sin_hbm, sin_ref),
        ))
    ]

    def peer_at(i):
        xi, zi = (i >> 1) & 3, i >> 3
        x_off = 2 + ((xi + 1) >> 1) * (1 - 2 * (xi & 1))
        z_off = 4 + ((zi + 1) >> 1) * (1 - 2 * (zi & 1))
        x_to = ((me >> 4) + x_off) & 3
        y_to = ((me >> 3) & 1) ^ (1 - (i & 1))
        z_to = (me + z_off) & 7
        return (x_to << 4) | (y_to << 3) | z_to

    def span(start, stop, body):
        def step(i, carry):
            body(peer_at(i))
            return carry

        lax.fori_loop(start, stop, step, 0, unroll=9)

    def peers(body):
        span(0, parts - 1, body)

    def target(peer):
        return dict(device_id=(peer, tp), device_id_type=pl.DeviceIdType.MESH)

    for load in loads[:6]:
        load.start()
    peers(lambda peer: pl.semaphore_signal(barrier, inc=1, **target(peer)))
    for load in loads[6:]:
        load.start()

    for load in loads[:6]:
        load.wait()

    def turned(ref):
        return jnp.transpose(ref[...].astype(F32)).reshape(parts, chans, rows)

    filt = turned(h_ref)
    peak = jnp.max(jnp.max(jnp.abs(filt), axis=2, keepdims=True), axis=1, keepdims=True)
    peak = jnp.broadcast_to(jnp.maximum(peak, TINY), (parts, 1, rows))
    peaks[...] = peak
    wave1[...] = jnp.concatenate([turned(q_ref), turned(v_ref), encode(filt * (RANGE / peak))], axis=1).astype(BF16)
    wave2[...] = jnp.concatenate([turned(k_ref), turned(g_ref)], axis=1).astype(BF16)
    taps = jnp.concatenate([taps_ref[0], taps_ref[1], taps_ref[2], jnp.zeros((rows - 9, width), F32)], axis=0)
    taps_t[...] = jnp.transpose(taps)

    pl.semaphore_wait(barrier, parts - 1)

    def keep(moves):
        for source, result, n, skip in moves:
            pltpu.make_async_copy(source.at[me + skip], result.at[me], recv_sem.at[n]).start()

    def post(peer, moves):
        for source, result, n, skip in moves:
            pltpu.make_async_remote_copy(
                src_ref=source.at[peer + skip], dst_ref=result.at[me],
                send_sem=send_sem.at[n], recv_sem=recv_sem.at[n], **target(peer)
            ).start()

    def exchange(moves):
        keep(moves)
        peers(lambda peer: post(peer, moves))

    def arrived(result, n):
        pltpu.make_async_copy(result, result, recv_sem.at[n]).wait()

    exchange([(peaks, got_peaks, 1, 0), (wave1, got1, 0, 0)])
    exchange([(wave2, got2, 2, 0)])
    arrived(got1, 0)
    arrived(got_peaks, 1)

    own_taps = taps_t[pl.ds(pl.multiple_of(me * chans, chans), chans), :]

    def tap(s, j):
        return jnp.broadcast_to(own_taps[:, 3 * s + j : 3 * s + j + 1], (chans, rows))[None]

    lane = lax.broadcasted_iota(jnp.int32, (1, chans, rows), 2)
    chunk = 8

    def rolled(value, shift):
        flat = value.reshape(-1, rows)
        return pltpu.roll(flat, shift % rows, axis=1).reshape(value.shape)

    x[:, 0] = jnp.zeros((4, chans, rows), F32)

    def unpack1(i, carry):
        p0 = i * chunk
        here = pl.ds(p0, chunk)
        there = pl.ds(p0 + 1, chunk)
        block = got1[here].astype(F32)
        x[0, there] = block[:, 0:8]
        x[2, there] = block[:, 8:16]
        fields[1, here] = decode(block[:, 16:24]) * (got_peaks[here] * (1.0 / RANGE))
        return carry

    def unpack2(i, carry):
        p0 = i * chunk
        there = pl.ds(p0 + 1, chunk)
        block = got2[pl.ds(p0, chunk)].astype(F32)
        x[1, there] = block[:, 0:8]
        x[3, there] = block[:, 8:16]
        return carry

    lax.fori_loop(0, parts // chunk, unpack1, 0, unroll=True)

    def delayed(s, p0):
        value = x[s, pl.ds(p0, chunk + 1)]
        out = [value[1:]]
        for j in (1, 2):
            moved = rolled(value, j)
            out.append(jnp.where(lane < j, moved[:-1], moved[1:]))
        return out

    def featured(s, p0):
        d = delayed(s, p0)
        here = pl.ds(p0, chunk)
        late[s, 0, here] = d[1]
        late[s, 1, here] = d[2]
        value = tap(s, 0) * d[0] + tap(s, 1) * d[1] + tap(s, 2) * d[2]
        feat[s, here] = value
        return value

    def featurize1(i, carry):
        p0 = i * chunk
        fields[0, pl.ds(p0, chunk)] = featured(0, p0) * featured(2, p0)
        return carry

    def featurize2(i, carry):
        p0 = i * chunk
        fields[2, pl.ds(p0, chunk)] = featured(1, p0) * x[3, pl.ds(p0 + 1, chunk)]
        return carry

    lax.fori_loop(0, parts // chunk, featurize1, 0, unroll=True)

    for load in loads[6:]:
        load.wait()
    turn_re, turn_im = cos_ref[...], sin_ref[...]
    first, second, last = first_ref[...], second_ref[...], last_ref[...]
    flat_fields = fields.reshape(3 * width, rows)
    flat_conv = conv.reshape(3 * width, rows)

    def twiddled(re, im):
        return re * turn_re - im * turn_im, re * turn_im + im * turn_re

    def forward(f):
        for c in range(0, chans, 2):
            pair = [flat_fields[pl.ds(f * width + c + e, parts, stride=chans), :] for e in (0, 1)]
            hi, lo = halves(jnp.concatenate(pair, axis=1))
            mid = jnp.dot(first, jnp.concatenate([hi, lo, hi], axis=0), preferred_element_type=F32)
            for e in (0, 1):
                re, im = twiddled(mid[:parts, e * rows : (e + 1) * rows], mid[parts:, e * rows : (e + 1) * rows])
                hi, lo = halves(jnp.concatenate([re, im], axis=1))
                lhs[f, (c + e) * parts : (c + e + 1) * parts, :] = jnp.concatenate([hi, lo, hi], axis=1)
        spec[f] = jnp.dot(lhs[f], second, preferred_element_type=F32)

    forward(0)
    forward(1)

    def inverse(o):
        f_a, f_b, sign = ((0, 1, 1.0), (2, 1, -1.0), (2, 0, -1.0))[o]
        for c in range(chans):
            block = pl.ds(c * parts, parts)
            a, b = spec[f_a, block, :], spec[f_b, block, :]
            a_re, a_im, b_re, b_im = a[:, :rows], a[:, rows:], b[:, :rows], sign * b[:, rows:]
            re, im = a_re * b_re - a_im * b_im, a_re * b_im + a_im * b_re
            hi, lo = halves(jnp.concatenate([re, -im], axis=1))
            lhs[o, c * parts : (c + 1) * parts, :] = jnp.concatenate([hi, lo, hi], axis=1)
        mid = jnp.dot(lhs[o], second, preferred_element_type=F32)
        for c in range(0, chans, 2):
            pair = []
            for e in (0, 1):
                block = mid[(c + e) * parts : (c + e + 1) * parts]
                pair.append(jnp.concatenate(twiddled(block[:, :rows], block[:, rows:]), axis=0))
            hi, lo = halves(jnp.concatenate(pair, axis=1))
            out = jnp.dot(last, jnp.concatenate([hi, lo, hi], axis=0), preferred_element_type=F32)
            for e in (0, 1):
                flat_conv[pl.ds(o * width + c + e, parts, stride=chans), :] = out[:, e * rows : (e + 1) * rows]

    def scaled(o):
        top = jnp.max(jnp.max(jnp.abs(conv[o]), axis=0), axis=1, keepdims=True)
        top = jnp.broadcast_to(jnp.maximum(top, TINY), (chans, rows))
        return top, (RANGE / top)[None]

    inverse(0)
    y_peak, y_gain = scaled(0)

    def code_y(i, carry):
        here = pl.ds(i * chunk, chunk)
        y_out[here] = encode(conv[0, here] * y_gain).astype(BF16)
        return carry

    lax.fori_loop(0, parts // chunk, code_y, 0, unroll=True)
    exchange([(y_out, y_in, 3, 0)])

    arrived(got2, 2)
    lax.fori_loop(0, parts // chunk, unpack2, 0, unroll=True)
    lax.fori_loop(0, parts // chunk, featurize2, 0, unroll=True)
    forward(2)
    inverse(1)
    inverse(2)
    dz_peak, dz_gain = scaled(1)
    dh_peak, dh_gain = scaled(2)
    peak = (y_peak, dz_peak, dh_peak)

    def code_d(i, carry):
        here = pl.ds(i * chunk, chunk)
        pair = [encode(conv[1, here] * dz_gain), encode(conv[2, here] * dh_gain)]
        d_out[here] = jnp.concatenate(pair, axis=1).astype(BF16)
        return carry

    lax.fori_loop(0, parts // chunk, code_d, 0, unroll=True)
    group = lax.broadcasted_iota(jnp.int32, (1, chans, rows), 2) // SLOTS
    sublane = lax.broadcasted_iota(jnp.int32, (1, chans, rows), 1)

    def flattened(value):
        for shift in (SLOTS, 2 * SLOTS, 4 * SLOTS):
            value = value + rolled(value, shift)
        return jnp.sum(jnp.where(group == sublane, value, 0.0), axis=1, keepdims=True)

    def placed(values, lane0):
        out = jnp.zeros_like(values[0])
        for n, value in enumerate(values):
            at = lane0 + 2 * n
            out = jnp.where((lane >= at) & (lane < at + 2), rolled(value, at) if at else value, out)
        return out

    def tally(i, sums):
        p0 = i * chunk
        here = pl.ds(p0, chunk)
        there = pl.ds(p0 + 1, chunk)
        y, dz = conv[0, here], conv[1, here]
        a = [feat[s, here] for s in range(3)]
        da = [dz * a[2], x[3, there] * y, dz * a[0]]
        sums = list(sums)
        for s in range(3):
            d = (x[s, there], late[s, 0, here], late[s, 1, here])
            for j in range(3):
                sums[3 * s + j] = sums[3 * s + j] + jnp.sum(da[s] * d[j], axis=0)
        notes_out[here, 0:1, :] = flattened(placed(da, 9))
        notes_out[there, 1:2, :] = flattened(placed(a, 0))
        return tuple(sums)

    sums = (jnp.zeros((chans, rows), F32),) * 9
    d_moves = [(d_out, d_in, 4, 0)]
    for i in range(parts // chunk):
        sums = tally(i, sums)
    notes_out[parts, 0:1, :] = jnp.zeros((1, rows), F32)
    lane2 = lane[0]
    first_note = jnp.zeros((chans, rows), F32)
    for n in range(9):
        first_note = jnp.where(lane2 == n, jnp.sum(sums[n], axis=1, keepdims=True), first_note)
    second_note = jnp.zeros((chans, rows), F32)
    for o in range(3):
        second_note = jnp.where(lane2 == 6 + o, peak[o], second_note)
    both = jnp.concatenate([flattened(first_note[None]), flattened(second_note[None])], axis=1)
    later = pl.ds(1, parts)
    notes_out[later] = notes_out[later] + both

    note_moves = [(notes_out, notes, 5, 1)]
    peers(lambda peer: post(peer, note_moves + d_moves))
    keep(d_moves + note_moves)
    arrived(y_in, 3)
    arrived(d_in, 4)
    arrived(notes, 5)
    for n, source in enumerate((wave1, peaks, wave2, y_out, d_out, notes_out)):
        sent = source.at[pl.ds(0, parts - 1)]
        pltpu.make_async_copy(sent, sent, send_sem.at[n]).wait()


def home_kernel(
    q_hbm, k_hbm, v_hbm, g_hbm, taps_hbm, y_hbm, d_hbm, notes_hbm,
    mixed_hbm, gq_hbm, gk_hbm, gv_hbm, gtaps_hbm, gh_hbm,
    q_ref, k_ref, v_ref, g_ref, taps_ref, y_ref, d_ref, notes_ref, load_sem,
    mixed_ref, gq_ref, gk_ref, gv_ref, gtaps_ref, gh_ref, store_sem,
    notes_t,
):
    parts, chans, rows = 64, 8, 128
    loads = [
        pltpu.make_async_copy(source, held, load_sem.at[n])
        for n, (source, held) in enumerate((
            (notes_hbm, notes_ref), (y_hbm, y_ref), (d_hbm, d_ref), (taps_hbm, taps_ref),
            (q_hbm, q_ref), (k_hbm, k_ref), (v_hbm, v_ref), (g_hbm, g_ref),
        ))
    ]
    for load in loads:
        load.start()
    results = (
        (gtaps_ref, gtaps_hbm), (gh_ref, gh_hbm), (mixed_ref, mixed_hbm), (gq_ref, gq_hbm), (gk_ref, gk_hbm), (gv_ref, gv_hbm),
    )
    stores = []
    loads[0].wait()
    for r in range(2):
        note = notes_ref[:, r, :]
        for c in range(chans):
            notes_t[r, pl.ds(c, parts, stride=chans), :] = pltpu.roll(note, (rows - SLOTS * c) % rows, axis=1) if c else note
    for load in loads[1:]:
        load.wait()
    row = lax.broadcasted_iota(jnp.int32, (rows, rows), 0)

    def put(b, n):
        held, result = results[n]
        block = (slice(None),) * (len(held.shape) - 1) + (slice(b * rows, (b + 1) * rows),)
        store = pltpu.make_async_copy(held.at[block], result.at[block], store_sem.at[b, n])
        store.start()
        stores.append(store)

    inputs = (q_ref, k_ref, v_ref)
    outputs = (gq_ref, gk_ref, gv_ref)
    pad = jnp.zeros((8, rows), F32)
    for b in range(4):
        cols = slice(b * rows, (b + 1) * rows)
        groups = slice(b * 16, (b + 1) * 16)
        note = [jnp.transpose(notes_t[r, cols, :])[0:16] for r in range(2)]
        for s in range(3):
            gtaps_ref[s, :, cols] = note[0][3 * s : 3 * s + 3]
        pair = decode(d_ref[groups].astype(F32))
        y, dz, dh = [
            jnp.transpose(value.reshape(rows, rows)) * (note[1][6 + o : 7 + o] * (1.0 / RANGE))
            for o, value in enumerate((decode(y_ref[groups].astype(F32)), pair[:, 0:8], pair[:, 8:16]))
        ]
        put(b, 0)
        gh_ref[:, cols] = dh
        put(b, 1)
        tap = [[taps_ref[s, j : j + 1, cols] for j in range(3)] for s in range(3)]
        a = []
        for s in range(3):
            value = inputs[s][:, cols].astype(F32)
            joined = jnp.concatenate([pad, value], axis=0)
            total = tap[s][0] * value + tap[s][1] * joined[7 : 7 + rows] + tap[s][2] * joined[6 : 6 + rows]
            total = jnp.where(row == 0, note[1][2 * s : 2 * s + 1], total)
            a.append(jnp.where(row == 1, note[1][2 * s + 1 : 2 * s + 2], total))
        mixed_ref[:, cols] = (a[1] * y).astype(BF16)
        put(b, 2)
        da = [dz * a[2], g_ref[:, cols].astype(F32) * y, dz * a[0]]
        for s in range(3):
            joined = jnp.concatenate([da[s], note[0][9 + 2 * s : 11 + 2 * s], pad[0:6]], axis=0)
            total = tap[s][0] * da[s] + tap[s][1] * joined[1 : 1 + rows] + tap[s][2] * joined[2 : 2 + rows]
            outputs[s][:, cols] = total.astype(BF16)
            put(b, 3 + s)
    for store in stores:
        store.wait()


def local(q_proj, k_proj, v_proj, short_taps, long_filter, grad_out):
    parts = lax.axis_size("ctx")
    rows, width = q_proj.shape
    chans = width // parts
    tables = [jnp.asarray(t) for t in make_tables(parts, rows)]
    hbm = pl.BlockSpec(memory_space=pltpu.HBM)
    field = [pltpu.VMEM((rows, width), BF16) for _ in range(4)]
    wide = [pltpu.VMEM((rows, width), F32)]
    taps = [pltpu.VMEM((3, 3, width), F32)]
    y_all = jax.ShapeDtypeStruct((parts, chans, rows), BF16)
    d_all = jax.ShapeDtypeStruct((parts, 2 * chans, rows), BF16)
    notes = jax.ShapeDtypeStruct((parts, 2, rows), F32)
    back = pl.pallas_call(
        sequence_kernel,
        out_shape=(y_all, d_all, notes),
        in_specs=[hbm] * 11,
        out_specs=(hbm,) * 3,
        scratch_shapes=[
            *[
                pltpu.VMEM((parts, 3 * chans, rows), BF16),
                pltpu.VMEM((parts, 2 * chans, rows), BF16),
                pltpu.VMEM((parts, 1, rows), F32),
            ] * 2,
            pltpu.VMEM(y_all.shape, BF16),
            pltpu.VMEM(d_all.shape, BF16),
            pltpu.VMEM((parts + 1, 2, rows), F32),
            pltpu.VMEM((width, rows), F32),
            pltpu.VMEM((4, parts + 1, chans, rows), F32),
            pltpu.VMEM((3, 2, parts, chans, rows), F32),
            pltpu.VMEM((3, parts, chans, rows), F32),
            pltpu.VMEM((3, parts, chans, rows), F32),
            pltpu.VMEM((3, width, 2 * rows), F32),
            pltpu.VMEM((3, parts, chans, rows), F32),
            pltpu.VMEM((3, width, 6 * rows), BF16),
            *[pltpu.SemaphoreType.DMA((6,))] * 2,
            *field,
            *wide,
            *taps,
            *[pltpu.VMEM(t.shape, t.dtype) for t in tables],
            pltpu.SemaphoreType.DMA((11,)),
        ],
        compiler_params=pltpu.CompilerParams(
            collective_id=0, has_side_effects=True, vmem_limit_bytes=63 << 20
        ),
        name="sequence_part",
    )(q_proj, k_proj, v_proj, grad_out, long_filter, short_taps, *tables)
    like = jax.ShapeDtypeStruct((rows, width), BF16)
    mixed, gq, gk, gv, gtaps, gh = pl.pallas_call(
        home_kernel,
        out_shape=(
            like, like, like, like,
            jax.ShapeDtypeStruct((3, 3, width), F32),
            jax.ShapeDtypeStruct((rows, width), F32),
        ),
        in_specs=[hbm] * 8,
        out_specs=(hbm,) * 6,
        scratch_shapes=[
            *field,
            *taps,
            *[pltpu.VMEM(value.shape, value.dtype) for value in back],
            pltpu.SemaphoreType.DMA((8,)),
            *field,
            *taps,
            *wide,
            pltpu.SemaphoreType.DMA((4, 6)),
            pltpu.VMEM((2, width, rows), F32),
        ],
        compiler_params=pltpu.CompilerParams(vmem_limit_bytes=63 << 20),
        name="home_part",
    )(q_proj, k_proj, v_proj, grad_out, short_taps, *back)
    return mixed, gq, gk, gv, gtaps, gh


def solution(mesh):
    field = P("ctx", "tp")
    taps = P(None, None, "tp")
    return jax.shard_map(
        local,
        mesh=mesh,
        in_specs=(field, field, field, taps, field, field),
        out_specs=(field, field, field, field, taps, field),
        check_vma=False,
    )
```
